256 devices in a mesh: tp: 4 (over x_lo, core), blk: 64 (over z, y, x_hi).
Axes of the slice: x: 4 (x_hi: 2, x_lo: 2; x = x_hi * 2 + x_lo), y: 4, z: 8, core: 2. Of those that a mesh axis runs over, the one named last changes fastest.
Arguments:
- query_feat: bfloat16 [16384, 768], P('blk', 'tp'), may hold values from -48 to 48
- key_feat: bfloat16 [16384, 768], P('blk', 'tp'), may hold values from -12 to 12
- head_weight: bfloat16 [768, 512], P('tp'), may hold values from -0.21875 to 0.21875
- pair: int32 [16384], P('blk'), may hold values from 0 to 16383, each once
Outputs:
- loss: float32 [], replicated
- grad_query: bfloat16 [16384, 768], P('blk', 'tp')
- grad_key: bfloat16 [16384, 768], P('blk', 'tp')
- grad_head: float32 [768, 512], P('tp')
The draws below stay inside these ranges and needn't reach their ends.
Inputs may be any that keep to these rules, and one draw needn't show every extreme that they name: pair is a permutation of the 16384 sample indices.
All inputs are finite; a program needn't handle non-finite values.
Results may differ from the reference program's by a relative error of at most 0.0079.
The reference program's roundings to bfloat16 on the way (of `zq`, `zk`, `weights`, `dzq` and `dzk`) count: a program that leaves them out, or rounds other values in their place, can miss the bound.
Values may be sent and summed in bfloat16 or wider, within the bound.
A program may use at most 64 MiB of HBM per device.

```python
import math
import jax
import jax.numpy as jnp
from jax import lax

DIN = 768
EMB = 512
ROWS_DEV = 256
BATCH = 16384


def feature_base(key, row_low, row_high):
    values = jnp.clip(jax.random.normal(key, (BATCH, DIN), jnp.float32), -6.0, 6.0)
    row_key = jax.random.fold_in(key, 11)
    row_scale = jnp.exp(jax.random.uniform(row_key, (BATCH, 1), jnp.float32, jnp.log(row_low), jnp.log(row_high)))
    return values * row_scale


def draw_key_feat(key, part):
    return feature_base(key, 1.0, 1.0).astype(jnp.bfloat16)


def draw_query_feat(key, part):
    own_key = jax.random.fold_in(key, 5)
    fresh = jnp.clip(jax.random.normal(own_key, (BATCH, DIN), jnp.float32), -6.0, 6.0)
    return fresh.astype(jnp.bfloat16)


def block_scale(key, extent, pieces, least, top_value):
    level, own = 1.0, jax.random.fold_in(key, 6)
    for position, shards_of in pieces:
        draws = jnp.exp(jax.random.uniform(jax.random.fold_in(own, position), (shards_of,), jnp.float32, least / len(pieces), top_value / len(pieces)))
        level = level * jnp.repeat(draws, extent[position] // shards_of).reshape([-1 if axis == position else 1 for axis in range(len(extent))])
    return level


def bell_draw(key, extent, width, limit, cuts=(), held_as=jnp.bfloat16):
    drawn = width * jax.random.normal(key, extent, jnp.float32)
    if cuts:
        drawn = drawn * block_scale(key, extent, cuts, -0.22, 0.18)
    return jnp.clip(drawn, -limit, limit).astype(held_as)


def setup_inputs(seed: int = 0) -> dict:
    splits = jax.random.split(jax.random.key(seed), 5)
    query_feat = draw_query_feat(jax.random.fold_in(splits[4], 71), 0)
    key_feat = draw_key_feat(jax.random.fold_in(splits[4], 71), 0)
    head_weight = bell_draw(splits[2], (DIN, EMB), DIN ** -0.5, 0.21875, ((0, 4),))
    pair = jax.random.permutation(splits[3], BATCH).astype(jnp.int32)
    return dict(query_feat=query_feat, key_feat=key_feat, head_weight=head_weight, pair=pair)


logit_gain = 3.0

def reference(query_feat, key_feat, head_weight, pair):
    zq = jnp.dot(query_feat, head_weight, preferred_element_type=jnp.float32).astype(jnp.bfloat16)
    zk = jnp.dot(key_feat, head_weight, preferred_element_type=jnp.float32).astype(jnp.bfloat16)
    batch_total = zq.shape[0]
    block_rows = ROWS_DEV
    block_count = batch_total // block_rows
    logit_scale = logit_gain / math.sqrt(EMB)
    key_blocks = zk.reshape(block_count, block_rows, EMB)
    starts = (jnp.arange(block_count) * block_rows).astype(jnp.int32)

    def forward_step(state_in, block):
        row_top, row_sum = state_in
        tile_scores = logit_scale * jnp.dot(zq, block.T, preferred_element_type=jnp.float32)
        new_top = jnp.maximum(row_top, lax.optimization_barrier(jnp.max(tile_scores, axis=1)))
        row_sum = row_sum * jnp.exp(row_top - new_top) + lax.optimization_barrier(jnp.sum(jnp.exp(tile_scores - new_top[:, None]), axis=1))
        return ((new_top, row_sum), None)
    init = (jnp.full((batch_total,), -1e+30, jnp.float32), jnp.zeros((batch_total,), jnp.float32))
    (row_top, row_sum), _ = lax.scan(forward_step, init, key_blocks)
    lse = row_top + jnp.log(row_sum)
    positive = logit_scale * lax.optimization_barrier(jnp.sum(zq.astype(jnp.float32) * zk[pair].astype(jnp.float32), axis=1))
    loss = jnp.mean(lse - positive)

    def backward_step(grad_rows, inputs):
        block, start_row = inputs
        tile_scores = logit_scale * jnp.dot(zq, block.T, preferred_element_type=jnp.float32)
        key_ids = start_row + jnp.arange(block_rows, dtype=jnp.int32)
        onehot = (pair[:, None] == key_ids[None, :]).astype(jnp.float32)
        weights = ((jnp.exp(tile_scores - lse[:, None]) - onehot) / batch_total).astype(jnp.bfloat16)
        grad_rows = grad_rows + logit_scale * jnp.dot(weights, block, preferred_element_type=jnp.float32)
        key_part = logit_scale * lax.dot_general(weights, zq, (((0,), (0,)), ((), ())), preferred_element_type=jnp.float32)
        return (grad_rows, key_part)
    grad_rows, key_parts = lax.scan(backward_step, jnp.zeros((batch_total, EMB), jnp.float32), (key_blocks, starts))
    dzq = grad_rows.astype(jnp.bfloat16)
    dzk = key_parts.reshape(batch_total, EMB).astype(jnp.bfloat16)
    grad_query = jnp.dot(dzq, head_weight.T, preferred_element_type=jnp.float32).astype(jnp.bfloat16)
    grad_key = jnp.dot(dzk, head_weight.T, preferred_element_type=jnp.float32).astype(jnp.bfloat16)
    grad_head = jnp.dot(query_feat.T, dzq, preferred_element_type=jnp.float32) + jnp.dot(key_feat.T, dzk, preferred_element_type=jnp.float32)
    return (loss, grad_query, grad_key, grad_head)
```

```python
import math

import jax
import jax.numpy as jnp
from jax import lax
from jax.sharding import Mesh, PartitionSpec as P

logit_gain = 3.0
TP = ("xlo", "core")
BLK = ("z", "y", "xh")
QG = ("z", "core")
KG = ("y", "xh", "xlo")


def body(query_feat, key_feat, head_weight, pair):
    rows = query_feat.shape[0]
    emb = head_weight.shape[1]
    tp_size = lax.axis_size(TP)
    quarter = rows // tp_size
    batch = rows * lax.axis_size(BLK)
    scale = logit_gain / math.sqrt(emb)
    tp_index = lax.axis_index(TP)
    zq_part = jnp.dot(query_feat, head_weight, preferred_element_type=jnp.float32)
    zk_part = jnp.dot(key_feat, head_weight, preferred_element_type=jnp.float32)
    zq_own = lax.psum_scatter(zq_part, TP, scatter_dimension=0, tiled=True).astype(jnp.bfloat16)
    zk_own = lax.psum_scatter(zk_part, TP, scatter_dimension=0, tiled=True).astype(jnp.bfloat16)
    pair_own = lax.dynamic_slice_in_dim(pair, tp_index * quarter, quarter, 0)
    zq = lax.all_gather(zq_own, QG, axis=0, tiled=True)
    zk = lax.all_gather(zk_own, KG, axis=0, tiled=True)
    pair_all = lax.all_gather(pair_own, QG, axis=0, tiled=True)
    local = jnp.arange(quarter, dtype=jnp.int32)
    ys = lax.axis_size("y")
    xhs = lax.axis_size("xh")
    xls = lax.axis_size("xlo")
    y_i = jnp.arange(ys, dtype=jnp.int32)[:, None, None, None]
    xh_i = jnp.arange(xhs, dtype=jnp.int32)[None, :, None, None]
    xl_i = jnp.arange(xls, dtype=jnp.int32)[None, None, :, None]
    z = lax.axis_index("z")
    core = lax.axis_index("core")
    cores = lax.axis_size("core")
    key_ids = (((z * ys + y_i) * xhs + xh_i) * rows + (xl_i * cores + core) * quarter + local).reshape(-1)
    scores = scale * lax.dot_general(zq, zk, (((1,), (1,)), ((), ())), preferred_element_type=jnp.float32)
    onehot = pair_all[:, None] == key_ids[None, :]
    top = jnp.max(scores, axis=1)
    expo = jnp.exp(scores - top[:, None])
    lse_part = top + jnp.log(jnp.sum(expo, axis=1))
    pos_part = jnp.sum(jnp.where(onehot, scores, 0.0))
    lse_parts = lax.all_gather(lse_part, QG, axis=0)
    lse = jax.nn.logsumexp(lse_parts, axis=0)
    loss_part = jnp.sum(lse) / lax.axis_size(QG) - pos_part
    weights = (jnp.exp(scores - lse[:, None]) - onehot.astype(jnp.float32)).astype(jnp.bfloat16)
    factor = scale / batch
    dzq_part = factor * jnp.dot(weights, zk, preferred_element_type=jnp.float32)
    dzk_part = factor * lax.dot_general(weights, zq, (((0,), (0,)), ((), ())), preferred_element_type=jnp.float32)
    dzq_own = lax.psum_scatter(dzq_part, QG, scatter_dimension=0, tiled=True).astype(jnp.bfloat16)
    dzk_own = lax.psum_scatter(dzk_part, KG, scatter_dimension=0, tiled=True).astype(jnp.bfloat16)
    dzq = lax.all_gather(dzq_own, TP, axis=0, tiled=True)
    dzk = lax.all_gather(dzk_own, TP, axis=0, tiled=True)
    back = (((1,), (1,)), ((), ()))
    grad_query = lax.dot_general(dzq, head_weight, back, preferred_element_type=jnp.float32).astype(jnp.bfloat16)
    grad_key = lax.dot_general(dzk, head_weight, back, preferred_element_type=jnp.float32).astype(jnp.bfloat16)
    rowd = (((0,), (0,)), ((), ()))
    head_part = lax.dot_general(query_feat, dzq, rowd, preferred_element_type=jnp.float32) + lax.dot_general(
        key_feat, dzk, rowd, preferred_element_type=jnp.float32
    )
    grad_head = lax.psum(head_part, BLK)
    loss = lax.psum(loss_part, BLK + TP) / batch
    return (loss, grad_query, grad_key, grad_head)


def solution(mesh):
    fine = Mesh(mesh.devices.reshape(2, 2, 8, 4, 2) if mesh.axis_names[0] == "tp" else
                mesh.devices.reshape(8, 4, 2, 2, 2),
                TP + BLK if mesh.axis_names[0] == "tp" else BLK + TP)
    in_specs = (P(BLK, TP), P(BLK, TP), P(TP, None), P(BLK))
    out_specs = (P(), P(BLK, TP), P(BLK, TP), P(TP, None))
    return jax.shard_map(body, mesh=fine, in_specs=in_specs, out_specs=out_specs, check_vma=False)
```

```python
import functools
import math

import jax
import jax.numpy as jnp
from jax import lax
from jax.experimental import pallas as pl
from jax.experimental.pallas import tpu as pltpu
from jax.sharding import Mesh, PartitionSpec as P

logit_gain = 3.0
TP = ("xlo", "core")
BLK = ("z", "y", "xh")
MESH = pl.DeviceIdType.MESH
F32 = jnp.float32
BF16 = jnp.bfloat16
NZ, NY, NX = 8, 4, 4
ROWS, OWN, EMB, FEAT = 256, 64, 512, 192
HALF = OWN // 2
BATCH = 16384
SCALE = logit_gain / math.sqrt(EMB)
N_SEMS = 144
NT = (((1,), (1,)), ((), ()))
TN = (((0,), (0,)), ((), ()))


def kernel(xq, xk, w, pair, loss_o, gq_o, gk_o, gh_o,
           fq, fk, wb, pbuf, zqa, zka, st, wt, lbuf,
           dqf, zs, zr, dk, ck, pk, k1, k2s, k2, dq4, dk4,
           gp, gs, g1r, g2r, g3r, l1, l2, l3, ss, rs):
    z, y, xh, xlo, c = [lax.axis_index(a) for a in ("z", "y", "xh", "xlo", "core")]
    x = 2 * xh + xlo
    t = 2 * xlo + c
    oc, oxlo, oxh = 1 - c, 1 - xlo, 1 - xh

    def at_z(d):
        return lax.rem(z + d, NZ)

    def at_y(d):
        return lax.rem(y + d, NY)

    def at_x(d):
        return lax.rem(x + d, NX)

    def dev_x(d):
        v = at_x(d)
        return {"xh": v // 2, "xlo": lax.rem(v, 2)}

    core_dev = {"core": oc}
    partner = {"xlo": oxlo}
    other = {"xlo": oxlo, "xh": oxh}
    cross = {"xlo": oxlo, "core": oc}
    z_dev = [{"z": at_z(d)} for d in range(NZ)]
    y_dev = [{"y": at_y(d)} for d in range(NY)]
    x_dev = [dev_x(d) for d in range(NX)]
    diag = [{"y": at_y(d), "xh": oxh} for d in range(NY)]

    peers = z_dev[1:] + y_dev[1:] + x_dev[1:] + diag[1:] + [core_dev, cross]
    barrier = pltpu.get_barrier_semaphore()
    for p in peers:
        pl.semaphore_signal(barrier, inc=1, device_id=p, device_id_type=MESH)
    pl.semaphore_wait(barrier, len(peers))

    copies = []

    def send(src, dst, dev):
        i = len(copies)
        cp = pltpu.make_async_remote_copy(src_ref=src, dst_ref=dst, send_sem=ss.at[i], recv_sem=rs.at[i],
                                          device_id=dev, device_id_type=MESH)
        cp.start()
        copies.append(cp)
        return cp

    def rows_of(a, b):
        return pl.ds((2 * a + b) * OWN, OWN)

    f2 = [send(r.at[rows_of(oxlo, c)], f.at[2], partner) for r, f in ((xq, fq), (xk, fk))]
    w2b = send(w.at[pl.ds(48, 144)], wb.at[2, pl.ds(48, 144)], other)
    f3 = [send(r.at[rows_of(oxlo, oc)], f.at[3], cross) for r, f in ((xq, fq), (xk, fk))]
    w2a = send(w.at[pl.ds(0, 48)], wb.at[2, pl.ds(0, 48)], partner)
    f1 = [send(r.at[rows_of(xlo, oc)], f.at[1], core_dev) for r, f in ((xq, fq), (xk, fk))]
    w1 = send(w, wb.at[1], core_dev)

    prow = pair[pl.ds(t, 1), :]
    pbuf[z] = jnp.concatenate([prow, prow], axis=1)
    pc = [send(pbuf.at[z], pbuf.at[z], z_dev[d]) for d in range(1, NZ)]

    own = rows_of(xlo, c)
    zq_acc = jnp.dot(xq[own, :], w[...], preferred_element_type=F32)
    zk_acc = jnp.dot(xk[own, :], w[...], preferred_element_type=F32)
    for cp in f1:
        cp.wait_recv()
    w1.wait_recv()
    zq_acc += jnp.dot(fq[1], wb[1], preferred_element_type=F32)
    zk_acc += jnp.dot(fk[1], wb[1], preferred_element_type=F32)
    w2a.wait_recv()
    w3a = send(wb.at[2, pl.ds(0, 48)], wb.at[3, pl.ds(0, 48)], core_dev)
    w2b.wait_recv()
    w3b = send(wb.at[2, pl.ds(48, 144)], wb.at[3, pl.ds(48, 144)], core_dev)
    for cp in f2:
        cp.wait_recv()
    zq_acc += jnp.dot(fq[2], wb[2], preferred_element_type=F32)
    zk_acc += jnp.dot(fk[2], wb[2], preferred_element_type=F32)
    for cp in f3:
        cp.wait_recv()
    w3a.wait_recv()
    w3b.wait_recv()
    zq_acc += jnp.dot(fq[3], wb[3], preferred_element_type=F32)
    zk_acc += jnp.dot(fk[3], wb[3], preferred_element_type=F32)
    zqa[z] = zq_acc.astype(BF16)
    zka[y, x, c] = zk_acc.astype(BF16)

    H = (pl.ds(0, HALF), pl.ds(HALF, HALF))
    up, down = z_dev[1], z_dev[NZ - 1]
    ring = {}
    for h in range(2):
        ring[0, 1, h] = send(zqa.at[z, H[h]], zqa.at[z, H[h]], up)
        ring[1, 1, h] = send(zqa.at[z, H[h]], zqa.at[z, H[h]], down)
    mine = zka.at[y, x, c]
    kx = [send(mine.at[H[0]], mine.at[H[0]], x_dev[d]) for d in range(1, NX)]
    ky = [send(mine.at[H[1]], mine.at[H[1]], y_dev[d]) for d in range(1, NY)]

    def ring_step(s):
        for h in range(2):
            for dr in range(2):
                if s == 5 or (s == 4 and h != dr):
                    continue
                ring[dr, s - 1, h].wait_recv()
                slab = at_z(NZ - s + 1) if dr == 0 else at_z(s - 1)
                ring[dr, s, h] = send(zqa.at[slab, H[h]], zqa.at[slab, H[h]], up if dr == 0 else down)

    ring_step(2)
    for cp in kx:
        cp.wait_recv()
    row0 = zka.at[y, :, c, H[0]]
    ky2 = [send(row0, row0, y_dev[d]) for d in range(1, NY)]
    for cp in ky:
        cp.wait_recv()
    col1 = zka.at[:, x, c, H[1]]
    kx2 = [send(col1, col1, x_dev[d]) for d in range(1, NX)]
    kc = [send(row0, row0, core_dev), send(col1, col1, core_dev)]
    ring_step(3)
    ring_step(4)
    for d in range(1, NY):
        ky2[d - 1].wait_recv()
        r = zka.at[at_y(NY - d), :, c, H[0]]
        kc.append(send(r, r, core_dev))
    for d in range(1, NX):
        kx2[d - 1].wait_recv()
        r = zka.at[:, at_x(NX - d), c, H[1]]
        kc.append(send(r, r, core_dev))
    for h in range(2):
        for dr in range(2):
            if h != dr:
                ring[dr, 3, h].wait_recv()
            else:
                ring[dr, 4, h].wait_recv()
    for cp in kc:
        cp.wait_recv()
    for cp in pc:
        cp.wait_recv()

    zq = zqa[...].reshape(NZ * OWN, EMB)

    def score_step(i, top):
        keys = zka[i // 2, pl.ds(lax.rem(i, 2) * 2, 2)].reshape(256, EMB)
        s = SCALE * lax.dot_general(keys, zq, NT, preferred_element_type=F32)
        st[i] = s
        return jnp.maximum(top, jnp.max(s, axis=0, keepdims=True))

    top = lax.fori_loop(0, 8, score_step, jnp.full((1, 512), -1e30, F32))

    def sum_step(i, total):
        return total + jnp.sum(jnp.exp(st[i] - top), axis=0, keepdims=True)

    total = lax.fori_loop(0, 8, sum_step, jnp.zeros((1, 512), F32))
    lbuf[z] = top + jnp.log(total)
    lc = [send(lbuf.at[z], lbuf.at[z], z_dev[d]) for d in range(1, NZ)]
    lane = lax.broadcasted_iota(jnp.int32, (1, 128), 1)
    pairs = jnp.concatenate([jnp.where(lane < 64, pbuf[2 * j], pbuf[2 * j + 1]) for j in range(4)], axis=1)
    pairs = pairs - z * 2048
    for cp in lc:
        cp.wait_recv()
    parts = [lbuf[i] for i in range(NZ)]
    lse_top = functools.reduce(jnp.maximum, parts)
    lse = lse_top + jnp.log(functools.reduce(jnp.add, [jnp.exp(p - lse_top) for p in parts]))

    key_iota = lax.broadcasted_iota(jnp.int32, (256, 512), 0)
    dqf[...] = jnp.zeros_like(dqf)

    def weight_step(i, pos):
        s = st[i]
        hit = (key_iota + i * 256) == pairs
        e = jnp.exp(s - lse)
        wt[i] = jnp.where(hit, e - 1.0, e).astype(BF16)
        keys = zka[i // 2, pl.ds(lax.rem(i, 2) * 2, 2)].reshape(256, EMB)
        dqf[...] += lax.dot_general(wt[i], keys, TN, preferred_element_type=F32).reshape(NZ, OWN, EMB)
        return pos + jnp.sum(jnp.where(hit, s, 0.0), axis=0, keepdims=True)

    pos = lax.fori_loop(0, 8, weight_step, jnp.zeros((1, 512), F32))
    lane5 = lax.broadcasted_iota(jnp.int32, (1, 512), 1)
    loss_row = jnp.where((lane5 >= z * OWN) & (lane5 < z * OWN + OWN), lse, 0.0) - pos
    loss_row = loss_row[:, 0:128] + loss_row[:, 128:256] + loss_row[:, 256:384] + loss_row[:, 384:512]

    FAC = SCALE / BATCH
    rz = {}

    def zred_step(s):
        for h in range(2):
            for dr in range(2):
                if s == 1 and h != dr:
                    continue
                dest = at_z(5 - s) if dr == 0 else at_z(NZ - 5 + s)
                v = dqf[dest, H[h], :] * FAC
                if s >= 3 or (s == 2 and h == dr):
                    rz[dr, s - 1, h].wait_recv()
                    v += zr[dr, s - 2, H[h], :].astype(F32)
                zs[dr, s - 1, H[h], :] = v.astype(BF16)
                rz[dr, s, h] = send(zs.at[dr, s - 1, H[h]], zr.at[dr, s - 1, H[h]], up if dr == 0 else down)

    zred_step(1)

    kcs = []
    for d in (1, 2, 3, 0):
        yy = at_y(d)

        def key_step(j, carry, yy=yy):
            g = jnp.dot(wt[yy * 2 + j], zq, preferred_element_type=F32) * FAC
            dk[yy, pl.ds(j * 2, 2)] = g.astype(BF16).reshape(2, 2, OWN, EMB)
            return carry

        lax.fori_loop(0, 2, key_step, 0)
        kcs.append((yy, send(dk.at[yy, :, oc], ck.at[yy], core_dev)))
        if d == 2:
            zred_step(2)
    for yy, cp in kcs:
        cp.wait_recv()
        pk[yy] = (dk[yy, :, c].astype(F32) + ck[yy].astype(F32)).astype(BF16)
    a1 = [send(pk.at[at_y(d), :, H[0]], k1.at[0, y], y_dev[d]) for d in range(1, NY)]
    b1 = [send(pk.at[:, at_x(d), H[1]], k1.at[1, x], x_dev[d]) for d in range(1, NX)]
    zred_step(3)
    zred_step(4)
    k1[0, y] = pk[y, :, H[0], :]
    k1[1, x] = pk[:, x, H[1], :]
    for cp in a1:
        cp.wait_recv()
    k2s[0] = functools.reduce(jnp.add, [k1[0, i].astype(F32) for i in range(4)]).astype(BF16)
    a2 = [send(k2s.at[0, at_x(d)], k2.at[0, x], x_dev[d]) for d in range(1, NX)]
    for cp in b1:
        cp.wait_recv()
    k2s[1] = functools.reduce(jnp.add, [k1[1, i].astype(F32) for i in range(4)]).astype(BF16)
    b2 = [send(k2s.at[1, at_y(d)], k2.at[1, y], y_dev[d]) for d in range(1, NY)]
    k2[0, x] = k2s[0, x]
    k2[1, y] = k2s[1, y]
    v = dqf[z] * FAC
    for dr in range(2):
        for h in range(2):
            rz[dr, 4, h].wait_recv()
        v += zr[dr, 3].astype(F32)
    dq4[t] = v.astype(BF16)
    l1[t] = loss_row
    tpt = 2 * oxlo + c
    q1 = send(dq4.at[t], dq4.at[t], partner)
    q2 = send(dq4.at[t], dq4.at[t], core_dev)
    lo1 = [send(l1.at[t], l1.at[t], p) for p in (core_dev, partner, cross)]
    for cp in a2 + b2:
        cp.wait_recv()
    for h in range(2):
        dk4[t, H[h], :] = functools.reduce(jnp.add, [k2[h, i].astype(F32) for i in range(4)]).astype(BF16)
    d1 = send(dk4.at[t], dk4.at[t], partner)
    d2 = send(dk4.at[t], dk4.at[t], core_dev)
    q1.wait_recv()
    q3 = send(dq4.at[tpt], dq4.at[tpt], core_dev)
    d1.wait_recv()
    d3 = send(dk4.at[tpt], dk4.at[tpt], core_dev)
    for cp in (q2, q3):
        cp.wait_recv()
    dq = dq4[...].reshape(ROWS, EMB)
    head = lax.dot_general(xq[...], dq, TN, preferred_element_type=F32)
    for cp in (d2, d3):
        cp.wait_recv()
    dkv = dk4[...].reshape(ROWS, EMB)
    head += lax.dot_general(xk[...], dkv, TN, preferred_element_type=F32)

    for i in range(4):
        for j in range(2):
            piece = head[i * 48:(i + 1) * 48, j * 256:(j + 1) * 256]
            gp[i, j] = piece
            gs[i, j] = piece.astype(BF16)
    for cp in lo1:
        cp.wait_recv()
    l2[y, xh] = l1[0] + l1[1] + l1[2] + l1[3]
    plane = [(y_dev[d], at_y(d), xh) for d in range(1, NY)] + [({"xh": oxh}, y, oxh)] + [
        (diag[d], at_y(d), oxh) for d in range(1, NY)]
    h1 = [send(gs.at[py, px], g1r.at[y, xh], p) for p, py, px in plane]
    lo2 = [send(l2.at[y, xh], l2.at[y, xh], p) for p, py, px in plane]
    gq_o[...] = lax.dot_general(dq, w[...], NT, preferred_element_type=F32).astype(BF16)
    gk_o[...] = lax.dot_general(dkv, w[...], NT, preferred_element_type=F32).astype(BF16)
    g1r[y, xh] = gs[y, xh]
    for cp in h1 + lo2:
        cp.wait_recv()
    order = [(i, j) for i in range(4) for j in range(2)]
    g2r[z] = functools.reduce(jnp.add, [g1r[i, j].astype(F32) for i, j in order]).astype(BF16)
    l3[z] = functools.reduce(jnp.add, [l2[i, j] for i, j in order])
    h2 = [send(g2r.at[z], g2r.at[z], z_dev[d]) for d in range(1, NZ)]
    lo3 = [send(l3.at[z], l3.at[z], z_dev[d]) for d in range(1, NZ)]
    for cp in h2 + lo3:
        cp.wait_recv()
    g3r[y, xh] = functools.reduce(jnp.add, [g2r[i].astype(F32) for i in range(NZ)])
    h3 = [send(g3r.at[y, xh], g3r.at[y, xh], p) for p, py, px in plane]
    row = functools.reduce(jnp.add, [l3[i] for i in range(NZ)])
    loss_o[...] = jnp.broadcast_to(jnp.sum(row, axis=1, keepdims=True) / BATCH, (1, 128))
    for cp in h3:
        cp.wait_recv()
    for i, j in order:
        gh_o[i * 48:(i + 1) * 48, j * 256:(j + 1) * 256] = g3r[i, j]
    for cp in copies:
        cp.wait_send()


def body(query_feat, key_feat, head_weight, pair):
    vmem = pl.BlockSpec(memory_space=pltpu.VMEM)
    V = pltpu.VMEM
    loss, gq, gk, gh = pl.pallas_call(
        kernel,
        out_shape=(
            jax.ShapeDtypeStruct((1, 128), F32),
            jax.ShapeDtypeStruct((ROWS, FEAT), BF16),
            jax.ShapeDtypeStruct((ROWS, FEAT), BF16),
            jax.ShapeDtypeStruct((FEAT, EMB), F32),
        ),
        in_specs=[vmem] * 4,
        out_specs=(vmem,) * 4,
        scratch_shapes=[
            V((4, OWN, FEAT), BF16), V((4, OWN, FEAT), BF16), V((4, FEAT, EMB), BF16),
            V((NZ, 1, 128), jnp.int32),
            V((NZ, OWN, EMB), BF16), V((NY, NX, 2, OWN, EMB), BF16),
            V((8, 256, 512), F32), V((8, 256, 512), BF16),
            V((NZ, 1, 512), F32),
            V((NZ, OWN, EMB), F32), V((2, 4, OWN, EMB), BF16), V((2, 4, OWN, EMB), BF16),
            V((NY, NX, 2, OWN, EMB), BF16), V((NY, NX, OWN, EMB), BF16), V((NY, NX, OWN, EMB), BF16),
            V((2, 4, 4, HALF, EMB), BF16), V((2, 4, HALF, EMB), BF16), V((2, 4, HALF, EMB), BF16),
            V((4, OWN, EMB), BF16), V((4, OWN, EMB), BF16),
            V((4, 2, 48, 256), F32), V((4, 2, 48, 256), BF16), V((4, 2, 48, 256), BF16),
            V((NZ, 48, 256), BF16), V((4, 2, 48, 256), F32),
            V((4, 1, 128), F32), V((4, 2, 1, 128), F32), V((NZ, 1, 128), F32),
            pltpu.SemaphoreType.DMA((N_SEMS,)), pltpu.SemaphoreType.DMA((N_SEMS,)),
        ],
        compiler_params=pltpu.CompilerParams(collective_id=0, has_side_effects=True, vmem_limit_bytes=48 << 20),
    )(query_feat, key_feat, head_weight, pair.reshape(4, OWN))
    return loss[0, 0], gq, gk, gh


def solution(mesh):
    shape = {"tp": (2, 2), "blk": (8, 4, 2)}
    names = {"tp": TP, "blk": BLK}
    a, b = mesh.axis_names
    fine = Mesh(mesh.devices.reshape(shape[a] + shape[b]), names[a] + names[b])
    in_specs = (P(BLK, TP), P(BLK, TP), P(TP, None), P(BLK))
    out_specs = (P(), P(BLK, TP), P(BLK, TP), P(TP, None))
    return jax.shard_map(body, mesh=fine, in_specs=in_specs, out_specs=out_specs, check_vma=False)
```

```python
import functools
import math

import jax
import jax.numpy as jnp
from jax import lax
from jax.experimental import pallas as pl
from jax.experimental.pallas import tpu as pltpu
from jax.sharding import Mesh, PartitionSpec as P

logit_gain = 3.0
TP = ("xlo", "core")
BLK = ("z", "y", "xh")
MESH = pl.DeviceIdType.MESH
F32 = jnp.float32
BF16 = jnp.bfloat16
NZ, NY, NX = 8, 4, 4
ROWS, OWN, EMB, FEAT = 256, 64, 512, 192
HALF = OWN // 2
BATCH = 16384
SCALE = logit_gain / math.sqrt(EMB)
N_SEMS = 192
NT = (((1,), (1,)), ((), ()))
TN = (((0,), (0,)), ((), ()))


OFF = (0, 1, 7, 2, 6, 3, 5, 4)
SLOT = {o: k for k, o in enumerate(OFF)}
FAR = (4, 3, 5, 2, 6, 1, 7)


def add_all(values):
    return functools.reduce(jnp.add, values)


def kernel(xq_h, xk_h, w_h, pair_h, loss_o, gq_h, gk_h, gh_o,
           xqt, xkt, xq, xk, w, pair, gq_v, gk_v, f, wb, pbuf, zqa, zka, st, wt, lbuf, lsum,
           dqf, zs, zr, dk, ck, pk, k1, k2s, k2, dq4, dk4,
           gs, g1r, g2r, g3s, g3r, l1, l2, l3, ss, rs, ls):
    z, y, xh, xlo, c = [lax.axis_index(a) for a in ("z", "y", "xh", "xlo", "core")]
    x = 2 * xh + xlo
    t = 2 * xlo + c
    oc, oxlo, oxh = 1 - c, 1 - xlo, 1 - xh

    loads = [pltpu.make_async_copy(a, b, ls.at[i]) for i, (a, b) in enumerate(
        ((xq_h, xqt), (xk_h, xkt), (w_h, w), (pair_h, pair)))]
    for cp in loads:
        cp.start()

    def at_z(d):
        return lax.rem(z + d, NZ)

    def at_y(d):
        return lax.rem(y + d, NY)

    def at_x(d):
        return lax.rem(x + d, NX)

    def dev_x(d):
        v = at_x(d)
        return {"xh": v // 2, "xlo": lax.rem(v, 2)}

    core_dev = {"core": oc}
    partner = {"xlo": oxlo}
    other = {"xlo": oxlo, "xh": oxh}
    cross = {"xlo": oxlo, "core": oc}
    z_dev = [{"z": at_z(d)} for d in range(NZ)]
    y_dev = [{"y": at_y(d)} for d in range(NY)]
    x_dev = [dev_x(d) for d in range(NX)]
    diag = [{"y": at_y(d), "xh": oxh} for d in range(NY)]

    peers = [z_dev[1], z_dev[7]] + y_dev[1:] + x_dev[1:] + [core_dev, cross]
    barrier = pltpu.get_barrier_semaphore()
    for p in peers:
        pl.semaphore_signal(barrier, inc=1, device_id=p, device_id_type=MESH)
    for cp in loads:
        cp.wait()
    xq[...] = xqt[...].T
    xk[...] = xkt[...].T
    pl.semaphore_wait(barrier, len(peers))

    copies = []

    def send(src, dst, dev):
        i = len(copies)
        cp = pltpu.make_async_remote_copy(src_ref=src, dst_ref=dst, send_sem=ss.at[i], recv_sem=rs.at[i],
                                          device_id=dev, device_id_type=MESH)
        cp.start()
        copies.append(cp)
        return cp

    def rows_of(a, b):
        return pl.ds((2 * a + b) * OWN, OWN)

    feats = ((xq, 0), (xk, 1))
    W = [pl.ds(48 * i, 48) for i in range(4)]
    f2 = [send(r.at[rows_of(oxlo, c)], f.at[2, i], partner) for r, i in feats]
    w2 = {i: send(w.at[W[i]], wb.at[2, W[i]], other) for i in (1, 2, 3)}
    f3 = [send(r.at[rows_of(oxlo, oc)], f.at[3, i], cross) for r, i in feats]
    w2[0] = send(w.at[W[0]], wb.at[2, W[0]], partner)
    f1 = [send(r.at[rows_of(xlo, oc)], f.at[1, i], core_dev) for r, i in feats]
    w1 = send(w, wb.at[1], core_dev)

    own = rows_of(xlo, c)

    def project(rows, weights):
        return jnp.dot(rows, weights, preferred_element_type=F32)

    acc = project(jnp.concatenate([xq[own, :], xk[own, :]], axis=0), w[...])
    for cp in f1:
        cp.wait_recv()
    w1.wait_recv()
    acc += project(f[1].reshape(2 * OWN, FEAT), wb[1])
    w3 = []
    for i in (1, 2, 0, 3):
        w2[i].wait_recv()
        w3.append(send(wb.at[2, W[i]], wb.at[3, W[i]], core_dev))
    for cp in f2:
        cp.wait_recv()
    acc += project(f[2].reshape(2 * OWN, FEAT), wb[2])
    for cp in f3 + w3:
        cp.wait_recv()
    acc += project(f[3].reshape(2 * OWN, FEAT), wb[3])
    zqa[0] = acc[:OWN].astype(BF16)
    zka[y, x, c] = acc[OWN:].astype(BF16)

    H = (pl.ds(0, HALF), pl.ds(HALF, HALF))
    ALL = pl.ds(0, OWN)
    up, down = z_dev[1], z_dev[NZ - 1]
    mine = zka.at[y, x, c]

    def ring_send(s, part=ALL):
        a, b = SLOT[(NZ - s + 1) % NZ], SLOT[s - 1]
        a2, b2 = SLOT[NZ - s], SLOT[s]
        pa, pb = (H[0], H[1]) if s == 4 else (ALL, ALL)
        return (send(zqa.at[a, pa], zqa.at[a2, pa], up), send(zqa.at[b, pb], zqa.at[b2, pb], down))

    NEAR = (2, 1, 3)
    r1 = ring_send(1)
    kx = {d: send(mine.at[H[0]], mine.at[H[0]], x_dev[d]) for d in NEAR}
    ky = {d: send(mine.at[H[1]], mine.at[H[1]], y_dev[d]) for d in NEAR}
    ky2 = {d: [] for d in NEAR}
    kx2 = {d: [] for d in NEAR}

    def spread_y(r):
        for d in NEAR:
            ky2[d].append(send(r, r, y_dev[d]))

    def spread_x(r):
        for d in NEAR:
            kx2[d].append(send(r, r, x_dev[d]))

    spread_y(mine.at[H[0]])
    spread_x(mine.at[H[1]])
    for cp in r1:
        cp.wait_recv()
    r2 = ring_send(2)
    for d in (1, 3, 2):
        kx[d].wait_recv()
        spread_y(zka.at[y, at_x(NX - d), c, H[0]])
        ky[d].wait_recv()
        spread_x(zka.at[at_y(NY - d), x, c, H[1]])
    row0 = zka.at[y, :, c, H[0]]
    col1 = zka.at[:, x, c, H[1]]
    kc = [send(row0, row0, core_dev), send(col1, col1, core_dev)]
    for cp in r2:
        cp.wait_recv()
    r3 = ring_send(3)
    for d in (1, 3):
        for cp in ky2[d]:
            cp.wait_recv()
        r = zka.at[at_y(NY - d), :, c, H[0]]
        kc.append(send(r, r, core_dev))
        for cp in kx2[d]:
            cp.wait_recv()
        r = zka.at[:, at_x(NX - d), c, H[1]]
        kc.append(send(r, r, core_dev))
    for cp in r3:
        cp.wait_recv()
    r4 = ring_send(4)
    for cp in ky2[2]:
        cp.wait_recv()
    r = zka.at[at_y(2), :, c, H[0]]
    kc.append(send(r, r, core_dev))
    for cp in kx2[2]:
        cp.wait_recv()
    r = zka.at[:, at_x(2), c, H[1]]
    kc.append(send(r, r, core_dev))
    for cp in kc:
        cp.wait_recv()

    def keys_at(i):
        return zka[i // 2, pl.ds(lax.rem(i, 2) * 2, 2)].reshape(256, EMB)

    def scores_of(g):
        q = zqa[pl.ds(4 * g, 4)].reshape(256, EMB)

        def score_step(i, top):
            s = SCALE * lax.dot_general(keys_at(i), q, NT, preferred_element_type=F32)
            st[g, i] = s
            return jnp.maximum(top, jnp.max(s, axis=0, keepdims=True))

        top = lax.fori_loop(0, 8, score_step, jnp.full((1, 256), -1e30, F32))

        def sum_step(i, total):
            return total + jnp.sum(jnp.exp(st[g, i] - top), axis=0, keepdims=True)

        return top + jnp.log(lax.fori_loop(0, 8, sum_step, jnp.zeros((1, 256), F32)))

    lane = lax.broadcasted_iota(jnp.int32, (1, 128), 1)
    low = lane < OWN

    def put_parts(g, row):
        for j in range(2):
            v = row[:, 128 * j:128 * j + 128]
            turned = pltpu.roll(v, OWN, 1)
            lbuf[z, at_z(OFF[4 * g + 2 * j])] = jnp.where(low, v, turned)
            lbuf[z, at_z(OFF[4 * g + 2 * j + 1])] = jnp.where(low, turned, v)

    put_parts(0, scores_of(0))
    for cp in r4:
        cp.wait_recv()
    put_parts(1, scores_of(1))
    lc = [send(lbuf.at[z], lbuf.at[z], z_dev[d]) for d in FAR]
    prow = pair[pl.ds(xlo, 1), :]
    pbuf[z] = jnp.where((lane // OWN) == c, prow, pltpu.roll(prow, OWN, 1))
    pc = [send(pbuf.at[z], pbuf.at[z], z_dev[d]) for d in FAR]
    key_iota = lax.broadcasted_iota(jnp.int32, (256, 256), 0)
    for cp in lc + pc:
        cp.wait_recv()
    for i in range(NZ):
        parts = [lbuf[k, i] for k in range(NZ)]
        m = functools.reduce(jnp.maximum, parts)
        lsum[i] = m + jnp.log(add_all([jnp.exp(p - m) for p in parts]))

    def in_order(at):
        return [jnp.concatenate([jnp.where(low, at(at_z(OFF[4 * g + 2 * j])), at(at_z(OFF[4 * g + 2 * j + 1])))
                                 for j in range(2)], axis=1) for g in range(2)]

    lse = in_order(lambda i: lsum[i])
    pairs = [p - z * 2048 for p in in_order(lambda i: pbuf[i])]

    FAC = SCALE / BATCH
    zq = zqa[...].reshape(NZ * OWN, EMB)
    a1, b1 = [], []

    def key_rows(yy, pos):
        def step(j, pos):
            i = yy * 2 + j
            new = []
            for g in range(2):
                s = st[g, i]
                hit = (key_iota + i * 256) == pairs[g]
                e = jnp.exp(s - lse[g])
                wt[i, :, 256 * g:256 * g + 256] = jnp.where(hit, e - 1.0, e).astype(BF16)
                new.append(pos[g] + jnp.sum(jnp.where(hit, s, 0.0), axis=0, keepdims=True))
            v = jnp.dot(wt[i], zq, preferred_element_type=F32) * FAC
            dk[yy, pl.ds(j * 2, 2)] = v.astype(BF16).reshape(2, 2, OWN, EMB)
            return tuple(new)

        return lax.fori_loop(0, 2, step, pos), send(dk.at[yy, :, oc], ck.at[yy], core_dev)

    def core_sum(d, cp):
        yy = at_y(d)
        cp.wait_recv()
        pk[yy] = (dk[yy, :, c].astype(F32) + ck[yy].astype(F32)).astype(BF16)
        if d:
            a1.append(send(pk.at[yy, :, H[0]], k1.at[0, y], y_dev[d]))
        for e in NEAR:
            b1.append(send(pk.at[yy, at_x(e), H[1]], k1.at[1, x, yy], x_dev[e]))

    pos = (jnp.zeros((1, 256), F32),) * 2
    pos, c2 = key_rows(at_y(2), pos)
    pos, c1 = key_rows(at_y(1), pos)
    core_sum(2, c2)
    pos, c3 = key_rows(at_y(3), pos)
    core_sum(1, c1)
    pos, c0 = key_rows(at_y(0), pos)
    core_sum(3, c3)

    def query_rows(g):
        wg = wt[:, :, 256 * g:256 * g + 256].reshape(2048, 256)
        v = lax.dot_general(wg, zka[...].reshape(2048, EMB), TN, preferred_element_type=F32) * FAC
        dqf[pl.ds(4 * g, 4)] = v.reshape(4, OWN, EMB)

    query_rows(1)
    def ahead(dr, d):
        return d if dr == 0 else NZ - d

    zc = {}
    for dr in range(2):
        zs[dr, 1, H[dr], :] = dqf[SLOT[4], H[dr], :].astype(BF16)
        zc[dr, 1] = send(zs.at[dr, 1, H[dr]], zr.at[dr, 1, H[dr]], z_dev[ahead(dr, 2)])
        zs[dr, 0] = dqf[SLOT[ahead(dr, 3)]].astype(BF16)
        zc[dr, 0] = send(zs.at[dr, 0], zr.at[dr, 0], z_dev[ahead(dr, 1)])
    core_sum(0, c0)
    k1[0, y] = pk[y, :, H[0], :]
    k1[1, x] = pk[:, x, H[1], :]
    query_rows(0)
    for dr in range(2):
        zs[dr, 2] = dqf[SLOT[ahead(dr, 1)]].astype(BF16)
        zc[dr, 2] = send(zs.at[dr, 2], zr.at[dr, 2], z_dev[ahead(dr, 1)])
    lanes0 = jnp.where(low, lse[0][:, :128], 0.0)
    l1[t] = lanes0 - add_all([p[:, 128 * j:128 * j + 128] for p in pos for j in range(2)])
    lo1 = [send(l1.at[t], l1.at[t], p) for p in (core_dev, partner, cross)]
    for dr in range(2):
        v = dqf[SLOT[ahead(dr, 2)]]
        zc[dr, 0].wait_recv()
        v += zr[dr, 0].astype(F32)
        zc[dr, 1].wait_recv()
        pieces = [v[:HALF], v[HALF:]]
        pieces[dr] += zr[dr, 1, H[dr], :].astype(F32)
        for h in range(2):
            zs[dr, 3, H[h], :] = pieces[h].astype(BF16)
        zc[dr, 3] = send(zs.at[dr, 3], zr.at[dr, 3], z_dev[ahead(dr, 2)])
    for cp in a1:
        cp.wait_recv()
    k2s[0] = add_all([k1[0, i].astype(F32) for i in range(4)]).astype(BF16)
    a2 = [send(k2s.at[0, at_x(d)], k2.at[0, x], x_dev[d]) for d in NEAR]
    for cp in b1:
        cp.wait_recv()
    k2s[1] = add_all([k1[1, i].astype(F32) for i in range(4)]).astype(BF16)
    b2 = [send(k2s.at[1, at_y(d)], k2.at[1, y], y_dev[d]) for d in NEAR]
    k2[0, x] = k2s[0, x]
    k2[1, y] = k2s[1, y]
    v = dqf[0]
    for dr in range(2):
        for i in (2, 3):
            zc[dr, i].wait_recv()
            v += zr[dr, i].astype(F32)
    dq4[t] = v.astype(BF16)
    tpt = 2 * oxlo + c
    q1 = send(dq4.at[t], dq4.at[t], partner)
    q2 = send(dq4.at[t], dq4.at[t], core_dev)
    for cp in a2 + b2:
        cp.wait_recv()
    for h in range(2):
        dk4[t, H[h], :] = add_all([k2[h, i].astype(F32) for i in range(4)]).astype(BF16)
    d1 = send(dk4.at[t], dk4.at[t], partner)
    d2 = send(dk4.at[t], dk4.at[t], core_dev)
    q1.wait_recv()
    q3 = send(dq4.at[tpt], dq4.at[tpt], core_dev)
    d1.wait_recv()
    d3 = send(dk4.at[tpt], dk4.at[tpt], core_dev)
    for cp in (q2, q3):
        cp.wait_recv()
    dq = dq4[...].reshape(ROWS, EMB)
    head = jnp.dot(xqt[...], dq, preferred_element_type=F32)
    for cp in (d2, d3):
        cp.wait_recv()
    dkv = dk4[...].reshape(ROWS, EMB)
    head += jnp.dot(xkt[...], dkv, preferred_element_type=F32)

    for i in range(4):
        for j in range(2):
            gs[i, j] = head[i * 48:(i + 1) * 48, j * 256:(j + 1) * 256].astype(BF16)
    plane = [(diag[2], at_y(2), oxh), (diag[1], at_y(1), oxh), (diag[3], at_y(3), oxh), (y_dev[2], at_y(2), xh),
             ({"xh": oxh}, y, oxh), (y_dev[1], at_y(1), xh), (y_dev[3], at_y(3), xh)]
    h1 = [send(gs.at[py, px], g1r.at[y, xh], p) for p, py, px in plane]
    for cp in lo1:
        cp.wait_recv()
    l2[y, xh] = l1[0] + l1[1] + l1[2] + l1[3]
    lo2 = [send(l2.at[y, xh], l2.at[y, xh], p) for p, py, px in plane]
    gq_v[...] = lax.dot_general(w[...], dq, NT, preferred_element_type=F32).astype(BF16)
    gk_v[...] = lax.dot_general(w[...], dkv, NT, preferred_element_type=F32).astype(BF16)
    stores = [pltpu.make_async_copy(a, b, ls.at[i]) for i, (a, b) in enumerate(((gq_v, gq_h), (gk_v, gk_h)))]
    for cp in stores:
        cp.start()
    g1r[y, xh] = gs[y, xh]
    for cp in h1:
        cp.wait_recv()
    order = [(i, j) for i in range(4) for j in range(2)]
    g2r[z] = add_all([g1r[i, j].astype(F32) for i, j in order]).astype(BF16)
    h2 = [send(g2r.at[z], g2r.at[z], z_dev[d]) for d in FAR]
    for cp in lo2:
        cp.wait_recv()
    l3[z] = add_all([l2[i, j] for i, j in order])
    lo3 = [send(l3.at[z], l3.at[z], z_dev[d]) for d in FAR]
    for cp in h2:
        cp.wait_recv()
    g3s[...] = add_all([g2r[i].astype(F32) for i in range(NZ)]).astype(BF16)
    g3r[y, xh] = g3s[...]
    h3 = [send(g3s, g3r.at[y, xh], p) for p, py, px in plane]
    for cp in lo3:
        cp.wait_recv()
    row = add_all([l3[i] for i in range(NZ)])
    loss_o[...] = jnp.broadcast_to(jnp.sum(row, axis=1, keepdims=True) / BATCH, (1, 128))
    for cp in h3:
        cp.wait_recv()
    for i, j in order:
        gh_o[i * 48:(i + 1) * 48, j * 256:(j + 1) * 256] = g3r[i, j].astype(F32)
    for cp in stores:
        cp.wait()
    for cp in copies:
        cp.wait_send()


def place(loss_h, a, b, d, loss_o, a_o, b_o, d_o, loss_v, a_v, b_v, d_v, sems):
    ins = ((d, d_v), (a, a_v), (b, b_v), (loss_h, loss_v))
    loads = [pltpu.make_async_copy(p, q, sems.at[i]) for i, (p, q) in enumerate(ins)]
    outs = ((d_v, d_o), (a_v, a_o), (b_v, b_o))
    stores = [pltpu.make_async_copy(p, q, sems.at[4 + i]) for i, (p, q) in enumerate(outs)]
    for cp in loads:
        cp.start()
    for i in range(3):
        loads[i].wait()
        stores[i].start()
    loads[3].wait()
    loss_o[...] = loss_v[:, 0:1]
    for cp in stores:
        cp.wait()


def body(query_feat, key_feat, head_weight, pair):
    vmem = pl.BlockSpec(memory_space=pltpu.VMEM)
    hbm = pl.BlockSpec(memory_space=pl.ANY)
    V = pltpu.VMEM
    loss, gq, gk, gh = pl.pallas_call(
        kernel,
        out_shape=(
            jax.ShapeDtypeStruct((1, 128), F32),
            jax.ShapeDtypeStruct((FEAT, ROWS), BF16),
            jax.ShapeDtypeStruct((FEAT, ROWS), BF16),
            jax.ShapeDtypeStruct((FEAT, EMB), F32),
        ),
        in_specs=[hbm] * 4,
        out_specs=(vmem, hbm, hbm, vmem),
        scratch_shapes=[
            V((FEAT, ROWS), BF16), V((FEAT, ROWS), BF16),
            V((ROWS, FEAT), BF16), V((ROWS, FEAT), BF16), V((FEAT, EMB), BF16), V((2, 128), jnp.int32),
            V((FEAT, ROWS), BF16), V((FEAT, ROWS), BF16),
            V((4, 2, OWN, FEAT), BF16), V((4, FEAT, EMB), BF16),
            V((NZ, 1, 128), jnp.int32),
            V((NZ, OWN, EMB), BF16), V((NY, NX, 2, OWN, EMB), BF16),
            V((2, 8, 256, 256), F32), V((8, 256, 512), BF16),
            V((NZ, NZ, 1, 128), F32), V((NZ, 1, 128), F32),
            V((NZ, OWN, EMB), F32), V((2, 4, OWN, EMB), BF16), V((2, 4, OWN, EMB), BF16),
            V((NY, NX, 2, OWN, EMB), BF16), V((NY, NX, OWN, EMB), BF16), V((NY, NX, OWN, EMB), BF16),
            V((2, 4, 4, HALF, EMB), BF16), V((2, 4, HALF, EMB), BF16), V((2, 4, HALF, EMB), BF16),
            V((4, OWN, EMB), BF16), V((4, OWN, EMB), BF16),
            V((4, 2, 48, 256), BF16), V((4, 2, 48, 256), BF16),
            V((NZ, 48, 256), BF16), V((48, 256), BF16), V((4, 2, 48, 256), BF16),
            V((4, 1, 128), F32), V((4, 2, 1, 128), F32), V((NZ, 1, 128), F32),
            pltpu.SemaphoreType.DMA((N_SEMS,)), pltpu.SemaphoreType.DMA((N_SEMS,)), pltpu.SemaphoreType.DMA((4,)),
        ],
        compiler_params=pltpu.CompilerParams(collective_id=0, has_side_effects=True, vmem_limit_bytes=60 << 20),
    )(query_feat.T, key_feat.T, head_weight, pair.reshape(2, 128))
    loss, gq, gk, gh = pl.pallas_call(
        place,
        out_shape=(jax.ShapeDtypeStruct((1, 1), F32),) + tuple(
            jax.ShapeDtypeStruct(v.shape, v.dtype) for v in (gq, gk, gh)),
        in_specs=[hbm] * 4,
        out_specs=(vmem, hbm, hbm, hbm),
        scratch_shapes=[V(v.shape, v.dtype) for v in (loss, gq, gk, gh)] + [pltpu.SemaphoreType.DMA((8,))],
        compiler_params=pltpu.CompilerParams(vmem_limit_bytes=60 << 20),
    )(loss, gq, gk, gh)
    return loss.reshape(()), gq.T, gk.T, gh


def solution(mesh):
    shape = {"tp": (2, 2), "blk": (8, 4, 2)}
    names = {"tp": TP, "blk": BLK}
    a, b = mesh.axis_names
    fine = Mesh(mesh.devices.reshape(shape[a] + shape[b]), names[a] + names[b])
    in_specs = (P(BLK, TP), P(BLK, TP), P(TP, None), P(BLK))
    out_specs = (P(), P(BLK, TP), P(BLK, TP), P(TP, None))
    return jax.shard_map(body, mesh=fine, in_specs=in_specs, out_specs=out_specs, check_vma=False)
```

```python
import functools
import math

import jax
import jax.numpy as jnp
from jax import lax
from jax.experimental import pallas as pl
from jax.experimental.pallas import tpu as pltpu
from jax.sharding import Mesh, PartitionSpec as P

logit_gain = 3.0
TP = ("xlo", "core")
BLK = ("z", "y", "xh")
MESH = pl.DeviceIdType.MESH
F32 = jnp.float32
BF16 = jnp.bfloat16
NZ, NY, NX = 8, 4, 4
ROWS, OWN, EMB, FEAT = 256, 64, 512, 192
HALF = OWN // 2
BATCH = 16384
SCALE = logit_gain / math.sqrt(EMB)
N_SEMS = 192
NT = (((1,), (1,)), ((), ()))
TN = (((0,), (0,)), ((), ()))


OFF = (0, 1, 7, 2, 6, 3, 5, 4)
SLOT = {o: k for k, o in enumerate(OFF)}
FAR = (4, 3, 5, 2, 6, 1, 7)


def add_all(values):
    return functools.reduce(jnp.add, values)


def kernel(xq_h, xk_h, w_h, pair_h, loss_o, gq_h, gk_h, gh_o,
           xqt, xkt, xq, xk, w, pair, f, wb, pbuf, zqa, zka, st, wt, lbuf, lsum,
           dqf, zs, zr, dk, ck, pk, k1, k2s, k2, dq4, dk4,
           gs, g1r, g2r, g3s, g3r, l1, l2, l3, ss, rs, ls):
    z, y, xh, xlo, c = [lax.axis_index(a) for a in ("z", "y", "xh", "xlo", "core")]
    x = 2 * xh + xlo
    t = 2 * xlo + c
    oc, oxlo, oxh = 1 - c, 1 - xlo, 1 - xh

    loads = [pltpu.make_async_copy(a, b, ls.at[i]) for i, (a, b) in enumerate(
        ((xq_h, xqt), (xk_h, xkt), (w_h, w), (pair_h, pair)))]
    for cp in loads:
        cp.start()

    def at_z(d):
        return lax.rem(z + d, NZ)

    def at_y(d):
        return lax.rem(y + d, NY)

    def at_x(d):
        return lax.rem(x + d, NX)

    def dev_x(d):
        v = at_x(d)
        return {"xh": v // 2, "xlo": lax.rem(v, 2)}

    core_dev = {"core": oc}
    partner = {"xlo": oxlo}
    other = {"xlo": oxlo, "xh": oxh}
    cross = {"xlo": oxlo, "core": oc}
    z_dev = [{"z": at_z(d)} for d in range(NZ)]
    y_dev = [{"y": at_y(d)} for d in range(NY)]
    x_dev = [dev_x(d) for d in range(NX)]
    diag = [{"y": at_y(d), "xh": oxh} for d in range(NY)]

    peers = [z_dev[1], z_dev[7]] + y_dev[1:] + x_dev[1:] + [core_dev, cross]
    barrier = pltpu.get_barrier_semaphore()
    for p in peers:
        pl.semaphore_signal(barrier, inc=1, device_id=p, device_id_type=MESH)
    for cp in loads:
        cp.wait()
    xq[...] = xqt[...].T
    xk[...] = xkt[...].T
    pl.semaphore_wait(barrier, len(peers))

    copies = []
    settled = [0]

    def settle(upto):
        for cp in copies[settled[0]:upto]:
            cp.wait_send()
        settled[0] = upto

    def send(src, dst, dev):
        i = len(copies)
        cp = pltpu.make_async_remote_copy(src_ref=src, dst_ref=dst, send_sem=ss.at[i], recv_sem=rs.at[i],
                                          device_id=dev, device_id_type=MESH)
        cp.start()
        copies.append(cp)
        return cp

    def rows_of(a, b):
        return pl.ds((2 * a + b) * OWN, OWN)

    feats = ((xq, 0), (xk, 1))
    W = [pl.ds(48 * i, 48) for i in range(4)]
    f2 = [send(r.at[rows_of(oxlo, c)], f.at[2, i], partner) for r, i in feats]
    w2 = {i: send(w.at[W[i]], wb.at[2, W[i]], other) for i in (1, 2, 3)}
    f3 = [send(r.at[rows_of(oxlo, oc)], f.at[3, i], cross) for r, i in feats]
    w2[0] = send(w.at[W[0]], wb.at[2, W[0]], partner)
    f1 = [send(r.at[rows_of(xlo, oc)], f.at[1, i], core_dev) for r, i in feats]
    w1 = send(w, wb.at[1], core_dev)

    own = rows_of(xlo, c)

    def project(rows, weights):
        return jnp.dot(rows, weights, preferred_element_type=F32)

    acc = project(jnp.concatenate([xq[own, :], xk[own, :]], axis=0), w[...])
    for cp in f1:
        cp.wait_recv()
    w1.wait_recv()
    acc += project(f[1].reshape(2 * OWN, FEAT), wb[1])
    w3 = []
    for i in (1, 2, 0, 3):
        w2[i].wait_recv()
        w3.append(send(wb.at[2, W[i]], wb.at[3, W[i]], core_dev))
    for cp in f2:
        cp.wait_recv()
    acc += project(f[2].reshape(2 * OWN, FEAT), wb[2])
    for cp in f3 + w3:
        cp.wait_recv()
    acc += project(f[3].reshape(2 * OWN, FEAT), wb[3])
    zqa[0] = acc[:OWN].astype(BF16)
    zka[0, y, c, x] = acc[OWN:OWN + HALF].astype(BF16)
    zka[1, x, c, y] = acc[OWN + HALF:].astype(BF16)

    H = (pl.ds(0, HALF), pl.ds(HALF, HALF))
    ALL = pl.ds(0, OWN)
    up, down = z_dev[1], z_dev[NZ - 1]
    home = (y, x)
    mine = (zka.at[0, y, c, x], zka.at[1, x, c, y])

    def ring_send(s, part=ALL):
        a, b = SLOT[(NZ - s + 1) % NZ], SLOT[s - 1]
        a2, b2 = SLOT[NZ - s], SLOT[s]
        pa, pb = (H[0], H[1]) if s == 4 else (ALL, ALL)
        return (send(zqa.at[a, pa], zqa.at[a2, pa], up), send(zqa.at[b, pb], zqa.at[b2, pb], down))

    NEAR = (2, 1, 3)
    r1 = ring_send(1)
    first = (x_dev, y_dev)
    second = (y_dev, x_dev)
    turn = (at_y, at_x)
    k1st = [{d: send(mine[h], mine[h], first[h][d]) for d in NEAR} for h in range(2)]
    k2nd = [{d: [] for d in NEAR} for h in range(2)]

    def spread(h, r):
        for d in NEAR:
            k2nd[h][d].append(send(r, r, second[h][d]))

    kc = {}

    def to_core(d):
        for h in range(2):
            for cp in k2nd[h][d] if d else ():
                cp.wait_recv()
            r = zka.at[h, turn[h](4 - d), c]
            kc[d, h] = send(r, r, core_dev)

    stats = ([], [])

    def score(d, g):
        q = zqa[pl.ds(4 * g, 4)].reshape(256, EMB)
        for h in range(2):
            a = turn[h](4 - d)
            v = SCALE * lax.dot_general(zka[h, a].reshape(256, EMB), q, NT, preferred_element_type=F32)
            m = jnp.max(v, axis=0, keepdims=True)
            st[g, h * 4 + a] = v
            stats[g].append((m, jnp.sum(jnp.exp(v - m), axis=0, keepdims=True)))

    def from_core(d):
        for h in range(2):
            kc[d, h].wait_recv()

    def merged(g):
        m = functools.reduce(jnp.maximum, [p[0] for p in stats[g]])
        return m + jnp.log(add_all([p[1] * jnp.exp(p[0] - m) for p in stats[g]]))

    lane = lax.broadcasted_iota(jnp.int32, (1, 128), 1)
    low = lane < OWN

    def put_parts(g, row):
        for j in range(2):
            v = row[:, 128 * j:128 * j + 128]
            turned = pltpu.roll(v, OWN, 1)
            lbuf[z, at_z(OFF[4 * g + 2 * j])] = jnp.where(low, v, turned)
            lbuf[z, at_z(OFF[4 * g + 2 * j + 1])] = jnp.where(low, turned, v)

    for h in range(2):
        spread(h, mine[h])
    for cp in r1:
        cp.wait_recv()
    r2 = ring_send(2)
    for d in (1, 3, 2):
        for h in range(2):
            k1st[h][d].wait_recv()
            b = turn[1 - h](4 - d)
            spread(h, zka.at[h, home[h], c, b])
    to_core(0)
    for cp in r2:
        cp.wait_recv()
    r3 = ring_send(3)
    from_core(0)
    score(0, 0)
    to_core(1)
    for cp in r3:
        cp.wait_recv()
    r4 = ring_send(4)
    to_core(3)
    from_core(1)
    score(1, 0)
    to_core(2)
    from_core(3)
    score(3, 0)
    for cp in r4:
        cp.wait_recv()
    for d in (0, 1, 3):
        score(d, 1)
    from_core(2)
    score(2, 0)
    score(2, 1)
    put_parts(0, merged(0))
    put_parts(1, merged(1))
    sent = len(copies)
    lc = [send(lbuf.at[z], lbuf.at[z], z_dev[d]) for d in FAR]
    prow = pair[pl.ds(xlo, 1), :]
    pbuf[z] = jnp.where((lane // OWN) == c, prow, pltpu.roll(prow, OWN, 1))
    pc = [send(pbuf.at[z], pbuf.at[z], z_dev[d]) for d in FAR]
    settle(sent)
    for cp in lc + pc:
        cp.wait_recv()
    for i in range(NZ):
        parts = [lbuf[k, i] for k in range(NZ)]
        m = functools.reduce(jnp.maximum, parts)
        lsum[i] = m + jnp.log(add_all([jnp.exp(p - m) for p in parts]))

    def in_order(at):
        return [jnp.concatenate([jnp.where(low, at(at_z(OFF[4 * g + 2 * j])), at(at_z(OFF[4 * g + 2 * j + 1])))
                                 for j in range(2)], axis=1) for g in range(2)]

    lse = in_order(lambda i: lsum[i])
    pairs = [p - z * 2048 for p in in_order(lambda i: pbuf[i])]

    FAC = SCALE / BATCH
    zq = zqa[...].reshape(NZ * OWN, EMB)
    row = lax.broadcasted_iota(jnp.int32, (256, 256), 0)
    core_row = (row // 128) * 64 + row % 32
    peer_row = (row // 32) % 4
    pos = (jnp.zeros((1, 256), F32),) * 2
    for h in range(2):
        ids = core_row + peer_row * (128, 512)[h] + 32 * h

        def weight_step(a, pos, h=h, ids=ids):
            new = []
            for g in range(2):
                v = st[g, h * 4 + a]
                hit = ids == pairs[g] - a * (512, 128)[h]
                e = jnp.exp(v - lse[g])
                wt[h * 4 + a, :, 256 * g:256 * g + 256] = jnp.where(hit, e - 1.0, e).astype(BF16)
                new.append(pos[g] + jnp.sum(jnp.where(hit, v, 0.0), axis=0, keepdims=True))
            return tuple(new)

        pos = lax.fori_loop(0, 4, weight_step, pos)

    def query_rows(g):
        wg = wt[:, :, 256 * g:256 * g + 256].reshape(2048, 256)
        v = lax.dot_general(wg, zka[...].reshape(2048, EMB), TN, preferred_element_type=F32) * FAC
        dqf[pl.ds(4 * g, 4)] = v.reshape(4, OWN, EMB)

    query_rows(1)
    def ahead(dr, d):
        return d if dr == 0 else NZ - d

    zc = {}
    for dr in range(2):
        zs[dr, 1, H[dr], :] = dqf[SLOT[4], H[dr], :].astype(BF16)
        zc[dr, 1] = send(zs.at[dr, 1, H[dr]], zr.at[dr, 1, H[dr]], z_dev[ahead(dr, 2)])
        zs[dr, 0] = dqf[SLOT[ahead(dr, 3)]].astype(BF16)
        zc[dr, 0] = send(zs.at[dr, 0], zr.at[dr, 0], z_dev[ahead(dr, 1)])

    kcs = {}

    def key_rows(d, h):
        a = turn[h](d)
        v = jnp.dot(wt[h * 4 + a], zq, preferred_element_type=F32) * FAC
        dk[h, a] = v.astype(BF16).reshape(2, 4, HALF, EMB)
        kcs[d, h] = send(dk.at[h, a, oc], ck.at[h, a], core_dev)

    k1c = ([], [])

    def core_sum(d, h):
        a = turn[h](d)
        kcs[d, h].wait_recv()
        v = (dk[h, a, c].astype(F32) + ck[h, a].astype(F32)).astype(BF16)
        if d:
            pk[h, a] = v
            k1c[h].append(send(pk.at[h, a], k1.at[h, home[h]], second[h][d]))
        else:
            k1[h, a] = v

    steps = [(d, h) for d in (2, 1, 3, 0) for h in range(2)]
    for n, (d, h) in enumerate(steps):
        key_rows(d, h)
        if n >= 3:
            core_sum(*steps[n - 3])
    for n in (5, 6, 7):
        core_sum(*steps[n])
    query_rows(0)
    for dr in range(2):
        zs[dr, 2] = dqf[SLOT[ahead(dr, 1)]].astype(BF16)
        zc[dr, 2] = send(zs.at[dr, 2], zr.at[dr, 2], z_dev[ahead(dr, 1)])
    lanes0 = jnp.where(low, lse[0][:, :128], 0.0)
    l1[t] = lanes0 - add_all([p[:, 128 * j:128 * j + 128] for p in pos for j in range(2)])
    lo1 = [send(l1.at[t], l1.at[t], p) for p in (core_dev, partner, cross)]
    for dr in range(2):
        v = dqf[SLOT[ahead(dr, 2)]]
        zc[dr, 0].wait_recv()
        v += zr[dr, 0].astype(F32)
        zc[dr, 1].wait_recv()
        pieces = [v[:HALF], v[HALF:]]
        pieces[dr] += zr[dr, 1, H[dr], :].astype(F32)
        for h in range(2):
            zs[dr, 3, H[h], :] = pieces[h].astype(BF16)
        zc[dr, 3] = send(zs.at[dr, 3], zr.at[dr, 3], z_dev[ahead(dr, 2)])
    k2c = []
    for h in range(2):
        for cp in k1c[h]:
            cp.wait_recv()
        k2s[h] = add_all([k1[h, i].astype(F32) for i in range(4)]).astype(BF16)
        me = home[1 - h]
        k2c += [send(k2s.at[h, turn[1 - h](d)], k2.at[h, me], first[h][d]) for d in NEAR]
        k2[h, me] = k2s[h, me]
    v = dqf[0]
    for dr in range(2):
        for i in (2, 3):
            zc[dr, i].wait_recv()
            v += zr[dr, i].astype(F32)
    dq4[t] = v.astype(BF16)
    tpt = 2 * oxlo + c
    q1 = send(dq4.at[t], dq4.at[t], partner)
    q2 = send(dq4.at[t], dq4.at[t], core_dev)
    d1, d2 = [], []
    for h in range(2):
        for cp in k2c[3 * h:3 * h + 3]:
            cp.wait_recv()
        dk4[t, H[h], :] = add_all([k2[h, i].astype(F32) for i in range(4)]).astype(BF16)
        r = dk4.at[t, H[h]]
        d1.append(send(r, r, partner))
        d2.append(send(r, r, core_dev))
    q1.wait_recv()
    q3 = send(dq4.at[tpt], dq4.at[tpt], core_dev)
    d3 = []
    for h in range(2):
        d1[h].wait_recv()
        r = dk4.at[tpt, H[h]]
        d3.append(send(r, r, core_dev))
    for cp in (q2, q3):
        cp.wait_recv()
    dq = dq4[...].reshape(ROWS, EMB)
    head = jnp.dot(xqt[...], dq, preferred_element_type=F32)
    for cp in d2 + d3:
        cp.wait_recv()
    dkv = dk4[...].reshape(ROWS, EMB)
    head += jnp.dot(xkt[...], dkv, preferred_element_type=F32)

    for i in range(4):
        for j in range(2):
            gs[i, j] = head[i * 48:(i + 1) * 48, j * 256:(j + 1) * 256].astype(BF16)
    plane = [(diag[2], at_y(2), oxh), (diag[1], at_y(1), oxh), (diag[3], at_y(3), oxh), (y_dev[2], at_y(2), xh),
             ({"xh": oxh}, y, oxh), (y_dev[1], at_y(1), xh), (y_dev[3], at_y(3), xh)]
    sent = len(copies)
    h1 = [send(gs.at[py, px], g1r.at[y, xh], p) for p, py, px in plane]
    for cp in lo1:
        cp.wait_recv()
    l2[y, xh] = l1[0] + l1[1] + l1[2] + l1[3]
    lo2 = [send(l2.at[y, xh], l2.at[y, xh], p) for p, py, px in plane]
    gq_h[...] = lax.dot_general(w[...], dq, NT, preferred_element_type=F32).astype(BF16)
    gk_h[...] = lax.dot_general(w[...], dkv, NT, preferred_element_type=F32).astype(BF16)
    g1r[y, xh] = gs[y, xh]
    settle(sent)
    for cp in h1:
        cp.wait_recv()
    order = [(i, j) for i in range(4) for j in range(2)]
    g2r[z] = add_all([g1r[i, j].astype(F32) for i, j in order]).astype(BF16)
    sent = len(copies)
    h2 = [send(g2r.at[z], g2r.at[z], z_dev[d]) for d in FAR]
    for cp in lo2:
        cp.wait_recv()
    l3[z] = add_all([l2[i, j] for i, j in order])
    lo3 = [send(l3.at[z], l3.at[z], z_dev[d]) for d in FAR]
    settle(sent)
    for cp in h2:
        cp.wait_recv()
    g3s[...] = add_all([g2r[i].astype(F32) for i in range(NZ)]).astype(BF16)
    g3r[y, xh] = g3s[...]
    sent = len(copies)
    h3 = [send(g3s, g3r.at[y, xh], p) for p, py, px in plane]
    for cp in lo3:
        cp.wait_recv()
    row = add_all([l3[i] for i in range(NZ)])
    loss_o[...] = jnp.broadcast_to(jnp.sum(row, axis=1, keepdims=True) / BATCH, (1, 128))
    settle(sent)
    for cp in h3:
        cp.wait_recv()
    for i, j in order:
        gh_o[i * 48:(i + 1) * 48, j * 256:(j + 1) * 256] = g3r[i, j].astype(F32)
    settle(len(copies))


def body(query_feat, key_feat, head_weight, pair):
    vmem = pl.BlockSpec(memory_space=pltpu.VMEM)
    hbm = pl.BlockSpec(memory_space=pl.ANY)
    V = pltpu.VMEM
    loss, gq, gk, gh = pl.pallas_call(
        kernel,
        out_shape=(
            jax.ShapeDtypeStruct((1, 128), F32),
            V((FEAT, ROWS), BF16),
            V((FEAT, ROWS), BF16),
            V((FEAT, EMB), F32),
        ),
        in_specs=[hbm] * 4,
        out_specs=(vmem, vmem, vmem, vmem),
        scratch_shapes=[
            V((FEAT, ROWS), BF16), V((FEAT, ROWS), BF16),
            V((ROWS, FEAT), BF16), V((ROWS, FEAT), BF16), V((FEAT, EMB), BF16), V((2, 128), jnp.int32),
            V((4, 2, OWN, FEAT), BF16), V((4, FEAT, EMB), BF16),
            V((NZ, 1, 128), jnp.int32),
            V((NZ, OWN, EMB), BF16), V((2, 4, 2, 4, HALF, EMB), BF16),
            V((2, 8, 256, 256), F32), V((8, 256, 512), BF16),
            V((NZ, NZ, 1, 128), F32), V((NZ, 1, 128), F32),
            V((NZ, OWN, EMB), F32), V((2, 4, OWN, EMB), BF16), V((2, 4, OWN, EMB), BF16),
            V((2, 4, 2, 4, HALF, EMB), BF16), V((2, 4, 4, HALF, EMB), BF16), V((2, 4, 4, HALF, EMB), BF16),
            V((2, 4, 4, HALF, EMB), BF16), V((2, 4, HALF, EMB), BF16), V((2, 4, HALF, EMB), BF16),
            V((4, OWN, EMB), BF16), V((4, OWN, EMB), BF16),
            V((4, 2, 48, 256), BF16), V((4, 2, 48, 256), BF16),
            V((NZ, 48, 256), BF16), V((48, 256), BF16), V((4, 2, 48, 256), BF16),
            V((4, 1, 128), F32), V((4, 2, 1, 128), F32), V((NZ, 1, 128), F32),
            pltpu.SemaphoreType.DMA((N_SEMS,)), pltpu.SemaphoreType.DMA((N_SEMS,)), pltpu.SemaphoreType.DMA((4,)),
        ],
        compiler_params=pltpu.CompilerParams(collective_id=0, has_side_effects=True, vmem_limit_bytes=44 << 20),
    )(*[pltpu.with_memory_space_constraint(v, pltpu.HBM) for v in (
        query_feat.T, key_feat.T, head_weight, pair.reshape(2, 128))])
    return loss[0, 0], gq.T, gk.T, gh


def solution(mesh):
    shape = {"tp": (2, 2), "blk": (8, 4, 2)}
    names = {"tp": TP, "blk": BLK}
    a, b = mesh.axis_names
    fine = Mesh(mesh.devices.reshape(shape[a] + shape[b]), names[a] + names[b])
    in_specs = (P(BLK, TP), P(BLK, TP), P(TP, None), P(BLK))
    out_specs = (P(), P(BLK, TP), P(BLK, TP), P(TP, None))
    return jax.shard_map(body, mesh=fine, in_specs=in_specs, out_specs=out_specs, check_vma=False)
```

```python
import functools
import math

import jax
import jax.numpy as jnp
from jax import lax
from jax.experimental import pallas as pl
from jax.experimental.pallas import tpu as pltpu
from jax.sharding import Mesh, PartitionSpec as P

logit_gain = 3.0
TP = ("xlo", "core")
BLK = ("z", "y", "xh")
MESH = pl.DeviceIdType.MESH
F32 = jnp.float32
BF16 = jnp.bfloat16
NZ, NY, NX = 8, 4, 4
ROWS, OWN, EMB, FEAT = 256, 64, 512, 192
HALF = OWN // 2
BATCH = 16384
SCALE = logit_gain / math.sqrt(EMB)
N_SEMS = 192
NT = (((1,), (1,)), ((), ()))
TN = (((0,), (0,)), ((), ()))


OFF = (0, 1, 7, 2, 6, 3, 5, 4)
SLOT = {o: k for k, o in enumerate(OFF)}
FAR = (4, 3, 5, 2, 6, 1, 7)


def add_all(values):
    return functools.reduce(jnp.add, values)


def kernel(xq_h, xk_h, w_h, pair_h, loss_o, gq_h, gk_h, gh_o,
           xqt, xkt, xq, xk, w, pair, f, wb, pbuf, zqa, zka, st, wt, lbuf, lsum,
           dqf, zs, zr, dk, ck, pk, k1, k2s, k2, dq4, dk4,
           gs, g1r, g2r, g3s, g3r, l1, l2, l3, ss, rs, ls):
    z, y, xh, xlo, c = [lax.axis_index(a) for a in ("z", "y", "xh", "xlo", "core")]
    x = 2 * xh + xlo
    t = 2 * xlo + c
    oc, oxlo, oxh = 1 - c, 1 - xlo, 1 - xh

    loads = [pltpu.make_async_copy(a, b, ls.at[i]) for i, (a, b) in enumerate(
        ((xq_h, xqt), (xk_h, xkt), (w_h, w), (pair_h, pair)))]
    for cp in loads:
        cp.start()

    def at_z(d):
        return lax.rem(z + d, NZ)

    def at_y(d):
        return lax.rem(y + d, NY)

    def at_x(d):
        return lax.rem(x + d, NX)

    def dev_x(d):
        v = at_x(d)
        return {"xh": v // 2, "xlo": lax.rem(v, 2)}

    core_dev = {"core": oc}
    partner = {"xlo": oxlo}
    other = {"xlo": oxlo, "xh": oxh}
    cross = {"xlo": oxlo, "core": oc}
    z_dev = [{"z": at_z(d)} for d in range(NZ)]
    y_dev = [{"y": at_y(d)} for d in range(NY)]
    x_dev = [dev_x(d) for d in range(NX)]
    diag = [{"y": at_y(d), "xh": oxh} for d in range(NY)]

    peers = [z_dev[1], z_dev[2], z_dev[6], z_dev[7]] + y_dev[1:] + x_dev[1:] + [core_dev, cross]
    barrier = pltpu.get_barrier_semaphore()
    for p in peers:
        pl.semaphore_signal(barrier, inc=1, device_id=p, device_id_type=MESH)
    for cp in loads:
        cp.wait()
    xq[...] = xqt[...].T
    xk[...] = xkt[...].T
    pl.semaphore_wait(barrier, len(peers))

    copies = []
    settled = [0]

    def settle(upto):
        for cp in copies[settled[0]:upto]:
            cp.wait_send()
        settled[0] = upto

    def send(src, dst, dev):
        i = len(copies)
        cp = pltpu.make_async_remote_copy(src_ref=src, dst_ref=dst, send_sem=ss.at[i], recv_sem=rs.at[i],
                                          device_id=dev, device_id_type=MESH)
        cp.start()
        copies.append(cp)
        return cp

    def rows_of(a, b):
        return pl.ds((2 * a + b) * OWN, OWN)

    feats = ((xq, 0), (xk, 1))
    W = [pl.ds(48 * i, 48) for i in range(4)]
    f2 = [send(r.at[rows_of(oxlo, c)], f.at[2, i], partner) for r, i in feats]
    w2 = {i: send(w.at[W[i]], wb.at[2, W[i]], other) for i in (1, 2, 3)}
    f3 = [send(r.at[rows_of(oxlo, oc)], f.at[3, i], cross) for r, i in feats]
    w2[0] = send(w.at[W[0]], wb.at[2, W[0]], partner)
    f1 = [send(r.at[rows_of(xlo, oc)], f.at[1, i], core_dev) for r, i in feats]
    w1 = send(w, wb.at[1], core_dev)

    own = rows_of(xlo, c)

    def project(rows, weights):
        return jnp.dot(rows, weights, preferred_element_type=F32)

    acc = project(jnp.concatenate([xq[own, :], xk[own, :]], axis=0), w[...])
    for cp in f1:
        cp.wait_recv()
    w1.wait_recv()
    acc += project(f[1].reshape(2 * OWN, FEAT), wb[1])
    w3 = []
    for i in (1, 2, 0, 3):
        w2[i].wait_recv()
        w3.append(send(wb.at[2, W[i]], wb.at[3, W[i]], core_dev))
    for cp in f2:
        cp.wait_recv()
    acc += project(f[2].reshape(2 * OWN, FEAT), wb[2])
    for cp in f3 + w3:
        cp.wait_recv()
    acc += project(f[3].reshape(2 * OWN, FEAT), wb[3])
    zqa[0] = acc[:OWN].astype(BF16)
    zka[0, y, c, x] = acc[OWN:OWN + HALF].astype(BF16)
    zka[1, x, c, y] = acc[OWN + HALF:].astype(BF16)

    H = (pl.ds(0, HALF), pl.ds(HALF, HALF))
    ALL = pl.ds(0, OWN)
    home = (y, x)
    mine = (zka.at[0, y, c, x], zka.at[1, x, c, y])

    def pass_on(k, part, d):
        return send(zqa.at[SLOT[k % NZ], part], zqa.at[SLOT[(k - d) % NZ], part], z_dev[d % NZ])

    NEAR = (2, 1, 3)
    r2 = [pass_on(0, ALL, d) for d in (2, -2)]
    r1 = [pass_on(0, ALL, d) for d in (1, -1)]
    first = (x_dev, y_dev)
    second = (y_dev, x_dev)
    turn = (at_y, at_x)
    k1st = [{d: send(mine[h], mine[h], first[h][d]) for d in NEAR} for h in range(2)]
    k2nd = [{d: [] for d in NEAR} for h in range(2)]

    def spread(h, r):
        for d in NEAR:
            k2nd[h][d].append(send(r, r, second[h][d]))

    kc = {}

    def to_core(d):
        for h in range(2):
            for cp in k2nd[h][d] if d else ():
                cp.wait_recv()
            r = zka.at[h, turn[h](4 - d), c]
            kc[d, h] = send(r, r, core_dev)

    stats = ([], [])

    def score(d, g):
        q = zqa[pl.ds(4 * g, 4)].reshape(256, EMB)
        for h in range(2):
            a = turn[h](4 - d)
            v = SCALE * lax.dot_general(zka[h, a].reshape(256, EMB), q, NT, preferred_element_type=F32)
            m = jnp.max(v, axis=0, keepdims=True)
            st[g, h * 4 + a] = v
            stats[g].append((m, jnp.sum(jnp.exp(v - m), axis=0, keepdims=True)))

    def from_core(d):
        for h in range(2):
            kc[d, h].wait_recv()

    def merged(g):
        m = functools.reduce(jnp.maximum, [p[0] for p in stats[g]])
        return m + jnp.log(add_all([p[1] * jnp.exp(p[0] - m) for p in stats[g]]))

    lane = lax.broadcasted_iota(jnp.int32, (1, 128), 1)
    low = lane < OWN

    def put_parts(g, row):
        for j in range(2):
            v = row[:, 128 * j:128 * j + 128]
            turned = pltpu.roll(v, OWN, 1)
            lbuf[z, pl.ds(at_z(OFF[4 * g + 2 * j]), 1), :] = jnp.where(low, v, turned)
            lbuf[z, pl.ds(at_z(OFF[4 * g + 2 * j + 1]), 1), :] = jnp.where(low, turned, v)

    for h in range(2):
        spread(h, mine[h])
    for d in (1, 3, 2):
        for h in range(2):
            k1st[h][d].wait_recv()
            b = turn[1 - h](4 - d)
            spread(h, zka.at[h, home[h], c, b])
    to_core(0)
    r4 = []
    for i, d in enumerate((1, -1)):
        r2[i].wait_recv()
        r4.append(pass_on(-2 * d, H[i], 2 * d))
        r4.append(pass_on(-2 * d, ALL, d))
    for cp in r1:
        cp.wait_recv()
    from_core(0)
    score(0, 0)
    to_core(1)
    to_core(3)
    from_core(1)
    score(1, 0)
    to_core(2)
    from_core(3)
    score(3, 0)
    for cp in r4:
        cp.wait_recv()
    prow = pair[pl.ds(xlo, 1), :]
    pbuf[z] = jnp.where((lane // OWN) == c, prow, pltpu.roll(prow, OWN, 1))
    pc = [send(pbuf.at[z], pbuf.at[z], z_dev[d]) for d in FAR]
    for d in (0, 1, 3):
        score(d, 1)
    from_core(2)
    score(2, 0)
    score(2, 1)
    put_parts(0, merged(0))
    put_parts(1, merged(1))
    sent = len(copies)
    lc = [send(lbuf.at[z], lbuf.at[z], z_dev[d]) for d in FAR]
    settle(sent)
    for cp in lc + pc:
        cp.wait_recv()
    parts = [lbuf[k] for k in range(NZ)]
    m = functools.reduce(jnp.maximum, parts)
    lsum[...] = m + jnp.log(add_all([jnp.exp(p - m) for p in parts]))

    def in_order(at):
        return [jnp.concatenate([jnp.where(low, at(at_z(OFF[4 * g + 2 * j])), at(at_z(OFF[4 * g + 2 * j + 1])))
                                 for j in range(2)], axis=1) for g in range(2)]

    lse = in_order(lambda i: lsum[pl.ds(i, 1), :])
    pairs = [p - z * 2048 for p in in_order(lambda i: pbuf[i])]

    FAC = SCALE / BATCH
    zq = zqa[...].reshape(NZ * OWN, EMB)
    row = lax.broadcasted_iota(jnp.int32, (256, 256), 0)
    core_row = (row // 128) * 64 + row % 32
    peer_row = (row // 32) % 4
    pos = []

    def weights_of(g):
        total = jnp.zeros((1, 256), F32)
        for h in range(2):
            ids = core_row + peer_row * (128, 512)[h] + 32 * h

            def weight_step(a, total, h=h, ids=ids):
                v = st[g, h * 4 + a]
                hit = ids == pairs[g] - a * (512, 128)[h]
                e = jnp.exp(v - lse[g])
                wt[h * 4 + a, :, 256 * g:256 * g + 256] = jnp.where(hit, e - 1.0, e).astype(BF16)
                return total + jnp.sum(jnp.where(hit, v, 0.0), axis=0, keepdims=True)

            total = lax.fori_loop(0, 4, weight_step, total)
        pos.append(total)

    weights_of(1)
    def query_rows(g):
        wg = wt[:, :, 256 * g:256 * g + 256].reshape(2048, 256)
        v = lax.dot_general(wg, zka[...].reshape(2048, EMB), TN, preferred_element_type=F32) * FAC
        dqf[pl.ds(4 * g, 4)] = v.reshape(4, OWN, EMB)

    query_rows(1)
    def ahead(dr, d):
        return d if dr == 0 else NZ - d

    zc = {}
    for dr in range(2):
        zs[dr, 1, H[dr], :] = dqf[SLOT[4], H[dr], :].astype(BF16)
        zc[dr, 1] = send(zs.at[dr, 1, H[dr]], zr.at[dr, 1, H[dr]], z_dev[ahead(dr, 2)])
    for n in range(2):
        for dr in range(2):
            h = H[1 - dr if n == 0 else dr]
            zs[dr, 0, h, :] = dqf[SLOT[ahead(dr, 3)], h, :].astype(BF16)
            zc[dr, 0, n] = send(zs.at[dr, 0, h], zr.at[dr, 0, h], z_dev[ahead(dr, 1)])
    weights_of(0)

    kcs = {}

    def key_rows(d, h):
        a = turn[h](d)
        v = jnp.dot(wt[h * 4 + a], zq, preferred_element_type=F32) * FAC
        dk[h, a] = v.astype(BF16).reshape(2, 4, HALF, EMB)
        kcs[d, h] = send(dk.at[h, a, oc], ck.at[h, a], core_dev)

    k1c = ([], [])

    def core_sum(d, h):
        a = turn[h](d)
        kcs[d, h].wait_recv()
        v = (dk[h, a, c].astype(F32) + ck[h, a].astype(F32)).astype(BF16)
        if d:
            pk[h, a] = v
            k1c[h].append(send(pk.at[h, a], k1.at[h, home[h]], second[h][d]))
        else:
            k1[h, a] = v

    steps = [(d, h) for d in (2, 1, 3, 0) for h in range(2)]
    for n, (d, h) in enumerate(steps):
        key_rows(d, h)
        if n >= 3:
            core_sum(*steps[n - 3])
    for n in (5, 6, 7):
        core_sum(*steps[n])
    query_rows(0)
    for dr in range(2):
        zs[dr, 2] = dqf[SLOT[ahead(dr, 1)]].astype(BF16)
        zc[dr, 2] = send(zs.at[dr, 2], zr.at[dr, 2], z_dev[ahead(dr, 1)])
    lanes0 = jnp.where(low, lse[0][:, :128], 0.0)
    l1[t] = lanes0 - add_all([p[:, 128 * j:128 * j + 128] for p in pos for j in range(2)])
    lo1 = [send(l1.at[t], l1.at[t], p) for p in (core_dev, partner, cross)]
    for n in range(2):
        for dr in range(2):
            h = H[1 - dr if n == 0 else dr]
            zc[dr, 0, n].wait_recv()
            v = dqf[SLOT[ahead(dr, 2)], h, :] + zr[dr, 0, h, :].astype(F32)
            if n == 1:
                zc[dr, 1].wait_recv()
                v += zr[dr, 1, h, :].astype(F32)
            zs[dr, 3, h, :] = v.astype(BF16)
            zc[dr, 3, n] = send(zs.at[dr, 3, h], zr.at[dr, 3, h], z_dev[ahead(dr, 2)])
    k2c = []
    for h in range(2):
        for cp in k1c[h]:
            cp.wait_recv()
        k2s[h] = add_all([k1[h, i].astype(F32) for i in range(4)]).astype(BF16)
        me = home[1 - h]
        k2c += [send(k2s.at[h, turn[1 - h](d)], k2.at[h, me], first[h][d]) for d in NEAR]
        k2[h, me] = k2s[h, me]
    tpt = 2 * oxlo + c
    for dr in range(2):
        zc[dr, 2].wait_recv()
    for n in range(2):
        for dr in range(2):
            zc[dr, 3, n].wait_recv()
    q1, q2 = [], []
    for h in range(2):
        dq4[t, H[h], :] = (dqf[0, H[h], :] + add_all(
            [zr[dr, i, H[h], :].astype(F32) for dr in range(2) for i in (2, 3)])).astype(BF16)
        r = dq4.at[t, H[h]]
        q1.append(send(r, r, partner))
        q2.append(send(r, r, core_dev))
    d1, d2 = [], []
    for h in range(2):
        for cp in k2c[3 * h:3 * h + 3]:
            cp.wait_recv()
        dk4[t, H[h], :] = add_all([k2[h, i].astype(F32) for i in range(4)]).astype(BF16)
        r = dk4.at[t, H[h]]
        d1.append(send(r, r, partner))
        d2.append(send(r, r, core_dev))
    q3 = []
    for h in range(2):
        q1[h].wait_recv()
        r = dq4.at[tpt, H[h]]
        q3.append(send(r, r, core_dev))
    d3 = []
    for h in range(2):
        d1[h].wait_recv()
        r = dk4.at[tpt, H[h]]
        d3.append(send(r, r, core_dev))
    for cp in q2 + q3:
        cp.wait_recv()
    dq = dq4[...].reshape(ROWS, EMB)
    head = jnp.dot(xqt[...], dq, preferred_element_type=F32)
    for cp in d2 + d3:
        cp.wait_recv()
    dkv = dk4[...].reshape(ROWS, EMB)
    head += jnp.dot(xkt[...], dkv, preferred_element_type=F32)

    for i in range(4):
        for j in range(2):
            gs[i, j] = head[i * 48:(i + 1) * 48, j * 256:(j + 1) * 256].astype(BF16)
    plane = [(diag[2], at_y(2), oxh), (diag[1], at_y(1), oxh), (diag[3], at_y(3), oxh), (y_dev[2], at_y(2), xh),
             ({"xh": oxh}, y, oxh), (y_dev[1], at_y(1), xh), (y_dev[3], at_y(3), xh)]
    sent = len(copies)
    h1 = [send(gs.at[py, px], g1r.at[y, xh], p) for p, py, px in plane]
    for cp in lo1:
        cp.wait_recv()
    l2[y, xh] = l1[0] + l1[1] + l1[2] + l1[3]
    lo2 = [send(l2.at[y, xh], l2.at[y, xh], p) for p, py, px in plane]
    gq_h[...] = lax.dot_general(w[...], dq, NT, preferred_element_type=F32).astype(BF16)
    gk_h[...] = lax.dot_general(w[...], dkv, NT, preferred_element_type=F32).astype(BF16)
    g1r[y, xh] = gs[y, xh]
    settle(sent)
    for cp in h1:
        cp.wait_recv()
    order = [(i, j) for i in range(4) for j in range(2)]
    g2r[z] = add_all([g1r[i, j].astype(F32) for i, j in order]).astype(BF16)
    sent = len(copies)
    h2 = [send(g2r.at[z], g2r.at[z], z_dev[d]) for d in FAR]
    for cp in lo2:
        cp.wait_recv()
    l3[z] = add_all([l2[i, j] for i, j in order])
    lo3 = [send(l3.at[z], l3.at[z], z_dev[d]) for d in FAR]
    settle(sent)
    for cp in h2:
        cp.wait_recv()
    g3s[...] = add_all([g2r[i].astype(F32) for i in range(NZ)]).astype(BF16)
    g3r[y, xh] = g3s[...]
    sent = len(copies)
    h3 = [send(g3s, g3r.at[y, xh], p) for p, py, px in plane]
    for cp in lo3:
        cp.wait_recv()
    row = add_all([l3[i] for i in range(NZ)])
    loss_o[...] = jnp.broadcast_to(jnp.sum(row, axis=1, keepdims=True) / BATCH, (1, 128))
    settle(sent)
    for cp in h3:
        cp.wait_recv()
    for i, j in order:
        gh_o[i * 48:(i + 1) * 48, j * 256:(j + 1) * 256] = g3r[i, j].astype(F32)
    settle(len(copies))


def body(query_feat, key_feat, head_weight, pair):
    vmem = pl.BlockSpec(memory_space=pltpu.VMEM)
    hbm = pl.BlockSpec(memory_space=pl.ANY)
    V = pltpu.VMEM
    loss, gq, gk, gh = pl.pallas_call(
        kernel,
        out_shape=(
            jax.ShapeDtypeStruct((1, 128), F32),
            V((FEAT, ROWS), BF16),
            V((FEAT, ROWS), BF16),
            V((FEAT, EMB), F32),
        ),
        in_specs=[hbm] * 4,
        out_specs=(vmem, vmem, vmem, vmem),
        scratch_shapes=[
            V((FEAT, ROWS), BF16), V((FEAT, ROWS), BF16),
            V((ROWS, FEAT), BF16), V((ROWS, FEAT), BF16), V((FEAT, EMB), BF16), V((2, 128), jnp.int32),
            V((4, 2, OWN, FEAT), BF16), V((4, FEAT, EMB), BF16),
            V((NZ, 1, 128), jnp.int32),
            V((NZ, OWN, EMB), BF16), V((2, 4, 2, 4, HALF, EMB), BF16),
            V((2, 8, 256, 256), F32), V((8, 256, 512), BF16),
            V((NZ, NZ, 128), F32), V((NZ, 128), F32),
            V((NZ, OWN, EMB), F32), V((2, 4, OWN, EMB), BF16), V((2, 4, OWN, EMB), BF16),
            V((2, 4, 2, 4, HALF, EMB), BF16), V((2, 4, 4, HALF, EMB), BF16), V((2, 4, 4, HALF, EMB), BF16),
            V((2, 4, 4, HALF, EMB), BF16), V((2, 4, HALF, EMB), BF16), V((2, 4, HALF, EMB), BF16),
            V((4, OWN, EMB), BF16), V((4, OWN, EMB), BF16),
            V((4, 2, 48, 256), BF16), V((4, 2, 48, 256), BF16),
            V((NZ, 48, 256), BF16), V((48, 256), BF16), V((4, 2, 48, 256), BF16),
            V((4, 1, 128), F32), V((4, 2, 1, 128), F32), V((NZ, 1, 128), F32),
            pltpu.SemaphoreType.DMA((N_SEMS,)), pltpu.SemaphoreType.DMA((N_SEMS,)), pltpu.SemaphoreType.DMA((4,)),
        ],
        compiler_params=pltpu.CompilerParams(collective_id=0, has_side_effects=True, vmem_limit_bytes=44 << 20),
    )(*[pltpu.with_memory_space_constraint(v, pltpu.HBM) for v in (
        query_feat.T, key_feat.T, head_weight, pair.reshape(2, 128))])
    return loss[0, 0], gq.T, gk.T, gh


def solution(mesh):
    shape = {"tp": (2, 2), "blk": (8, 4, 2)}
    names = {"tp": TP, "blk": BLK}
    a, b = mesh.axis_names
    fine = Mesh(mesh.devices.reshape(shape[a] + shape[b]), names[a] + names[b])
    in_specs = (P(BLK, TP), P(BLK, TP), P(TP, None), P(BLK))
    out_specs = (P(), P(BLK, TP), P(BLK, TP), P(TP, None))
    return jax.shard_map(body, mesh=fine, in_specs=in_specs, out_specs=out_specs, check_vma=False)
```

```python
import functools
import math

import jax
import jax.numpy as jnp
from jax import lax
from jax.experimental import pallas as pl
from jax.experimental.pallas import tpu as pltpu
from jax.sharding import Mesh, PartitionSpec as P

logit_gain = 3.0
TP = ("xlo", "core")
BLK = ("z", "y", "xh")
MESH = pl.DeviceIdType.MESH
F32 = jnp.float32
BF16 = jnp.bfloat16
NZ, NY, NX = 8, 4, 4
ROWS, OWN, EMB, FEAT = 256, 64, 512, 192
HALF = OWN // 2
BATCH = 16384
SCALE = logit_gain / math.sqrt(EMB)
N_SEMS = 192
NT = (((1,), (1,)), ((), ()))
TN = (((0,), (0,)), ((), ()))


OFF = (0, 1, 7, 2, 6, 3, 5, 4)
SLOT = {o: k for k, o in enumerate(OFF)}
FAR = (4, 3, 5, 2, 6, 1, 7)


def add_all(values):
    return functools.reduce(jnp.add, values)


def kernel(xq_h, xk_h, w_h, pair_h, loss_o, gq_h, gk_h, gh_o,
           xqt, xkt, xq, xk, w, pair, f, wb, pbuf, zqa, zka, st, wt, lbuf, lsum,
           dqf, zs, zr, dk, ck, pk, k1, k2s, k2, dq4, dk4,
           gs, g1r, g2r, g3s, g3r, l1, l2, l3, ss, rs, ls):
    z, y, xh, xlo, c = [lax.axis_index(a) for a in ("z", "y", "xh", "xlo", "core")]
    x = 2 * xh + xlo
    t = 2 * xlo + c
    oc, oxlo, oxh = 1 - c, 1 - xlo, 1 - xh

    loads = [pltpu.make_async_copy(a, b, ls.at[i]) for i, (a, b) in enumerate(
        ((xq_h, xqt), (xk_h, xkt), (w_h, w), (pair_h, pair)))]
    for cp in loads:
        cp.start()

    def at_z(d):
        return lax.rem(z + d, NZ)

    def at_y(d):
        return lax.rem(y + d, NY)

    def at_x(d):
        return lax.rem(x + d, NX)

    def dev_x(d):
        v = at_x(d)
        return {"xh": v // 2, "xlo": lax.rem(v, 2)}

    core_dev = {"core": oc}
    partner = {"xlo": oxlo}
    other = {"xlo": oxlo, "xh": oxh}
    cross = {"xlo": oxlo, "core": oc}
    z_dev = [{"z": at_z(d)} for d in range(NZ)]
    y_dev = [{"y": at_y(d)} for d in range(NY)]
    x_dev = [dev_x(d) for d in range(NX)]
    diag = [{"y": at_y(d), "xh": oxh} for d in range(NY)]

    peers = [z_dev[1], z_dev[2], z_dev[6], z_dev[7]] + y_dev[1:] + x_dev[1:] + [core_dev, cross]
    barrier = pltpu.get_barrier_semaphore()
    for p in peers:
        pl.semaphore_signal(barrier, inc=1, device_id=p, device_id_type=MESH)
    for cp in loads:
        cp.wait()
    xq[...] = xqt[...].T
    xk[...] = xkt[...].T
    pl.semaphore_wait(barrier, len(peers))

    copies = []
    settled = [0]

    def settle(upto):
        for cp in copies[settled[0]:upto]:
            cp.wait_send()
        settled[0] = upto

    def send(src, dst, dev):
        i = len(copies)
        cp = pltpu.make_async_remote_copy(src_ref=src, dst_ref=dst, send_sem=ss.at[i], recv_sem=rs.at[i],
                                          device_id=dev, device_id_type=MESH)
        cp.start()
        copies.append(cp)
        return cp

    def rows_of(a, b):
        return pl.ds((2 * a + b) * OWN, OWN)

    feats = ((xq, 0), (xk, 1))
    W = [pl.ds(48 * i, 48) for i in range(4)]
    f2 = [send(r.at[rows_of(oxlo, c)], f.at[2, i], partner) for r, i in feats]
    w2 = {i: send(w.at[W[i]], wb.at[2, W[i]], other) for i in (1, 2, 3)}
    f3 = [send(r.at[rows_of(oxlo, oc)], f.at[3, i], cross) for r, i in feats]
    w2[0] = send(w.at[W[0]], wb.at[2, W[0]], partner)
    f1 = [send(r.at[rows_of(xlo, oc)], f.at[1, i], core_dev) for r, i in feats]
    w1 = send(w, wb.at[1], core_dev)

    own = rows_of(xlo, c)

    def project(rows, weights):
        return jnp.dot(rows, weights, preferred_element_type=F32)

    acc = project(jnp.concatenate([xq[own, :], xk[own, :]], axis=0), w[...])
    for cp in f1:
        cp.wait_recv()
    w1.wait_recv()
    acc += project(f[1].reshape(2 * OWN, FEAT), wb[1])
    w3 = []
    for i in (1, 2, 0, 3):
        w2[i].wait_recv()
        w3.append(send(wb.at[2, W[i]], wb.at[3, W[i]], core_dev))
    for cp in f2:
        cp.wait_recv()
    acc += project(f[2].reshape(2 * OWN, FEAT), wb[2])
    for cp in f3 + w3:
        cp.wait_recv()
    acc += project(f[3].reshape(2 * OWN, FEAT), wb[3])
    zqa[0] = acc[:OWN].astype(BF16)
    zka[0, y, c, x] = acc[OWN:OWN + HALF].astype(BF16)
    zka[1, x, c, y] = acc[OWN + HALF:].astype(BF16)

    H = (pl.ds(0, HALF), pl.ds(HALF, HALF))
    ALL = pl.ds(0, OWN)
    home = (y, x)
    mine = (zka.at[0, y, c, x], zka.at[1, x, c, y])

    def pass_on(k, part, d):
        return send(zqa.at[SLOT[k % NZ], part], zqa.at[SLOT[(k - d) % NZ], part], z_dev[d % NZ])

    NEAR = (2, 1, 3)
    r2 = [pass_on(0, ALL, d) for d in (2, -2)]
    r1 = [pass_on(0, ALL, d) for d in (1, -1)]
    first = (x_dev, y_dev)
    second = (y_dev, x_dev)
    turn = (at_y, at_x)
    k1st = [{d: send(mine[h], mine[h], first[h][d]) for d in NEAR} for h in range(2)]
    k2nd = [{d: [] for d in NEAR} for h in range(2)]

    def spread(h, r):
        for d in NEAR:
            k2nd[h][d].append(send(r, r, second[h][d]))

    kc = {}

    def to_core(d):
        for h in range(2):
            for cp in k2nd[h][d] if d else ():
                cp.wait_recv()
            r = zka.at[h, turn[h](4 - d), c]
            kc[d, h] = send(r, r, core_dev)

    stats = ([], [])

    def score(d, g):
        q = zqa[pl.ds(4 * g, 4)].reshape(256, EMB)
        for h in range(2):
            a = turn[h](4 - d)
            v = SCALE * lax.dot_general(zka[h, a].reshape(256, EMB), q, NT, preferred_element_type=F32)
            m = jnp.max(v, axis=0, keepdims=True)
            st[g, h * 4 + a] = v
            stats[g].append((m, jnp.sum(jnp.exp(v - m), axis=0, keepdims=True)))

    def from_core(d):
        for h in range(2):
            kc[d, h].wait_recv()

    def merged(g):
        m = functools.reduce(jnp.maximum, [p[0] for p in stats[g]])
        return m + jnp.log(add_all([p[1] * jnp.exp(p[0] - m) for p in stats[g]]))

    lane = lax.broadcasted_iota(jnp.int32, (1, 128), 1)
    low = lane < OWN

    def put_parts(g, row):
        for j in range(2):
            v = row[:, 128 * j:128 * j + 128]
            turned = pltpu.roll(v, OWN, 1)
            lbuf[z, pl.ds(at_z(OFF[4 * g + 2 * j]), 1), :] = jnp.where(low, v, turned)
            lbuf[z, pl.ds(at_z(OFF[4 * g + 2 * j + 1]), 1), :] = jnp.where(low, turned, v)

    for h in range(2):
        spread(h, mine[h])
    for d in (1, 3, 2):
        for h in range(2):
            k1st[h][d].wait_recv()
            b = turn[1 - h](4 - d)
            spread(h, zka.at[h, home[h], c, b])
    to_core(0)
    r4 = []
    for i, d in enumerate((1, -1)):
        r2[i].wait_recv()
        r4.append(pass_on(-2 * d, H[i], 2 * d))
        r4.append(pass_on(-2 * d, ALL, d))
    for cp in r1:
        cp.wait_recv()
    from_core(0)
    score(0, 0)
    to_core(1)
    to_core(3)
    from_core(1)
    score(1, 0)
    to_core(2)
    from_core(3)
    score(3, 0)
    for cp in r4:
        cp.wait_recv()
    prow = pair[pl.ds(xlo, 1), :]
    pbuf[z] = jnp.where((lane // OWN) == c, prow, pltpu.roll(prow, OWN, 1))
    pc = [send(pbuf.at[z], pbuf.at[z], z_dev[d]) for d in FAR]
    for d in (0, 1, 3):
        score(d, 1)
    from_core(2)
    score(2, 0)
    score(2, 1)
    put_parts(0, merged(0))
    put_parts(1, merged(1))
    sent = len(copies)
    lc = [send(lbuf.at[z], lbuf.at[z], z_dev[d]) for d in FAR]
    settle(sent)
    for cp in lc + pc:
        cp.wait_recv()
    parts = [lbuf[k] for k in range(NZ)]
    m = functools.reduce(jnp.maximum, parts)
    lsum[...] = m + jnp.log(add_all([jnp.exp(p - m) for p in parts]))

    def in_order(at):
        return [jnp.concatenate([jnp.where(low, at(at_z(OFF[4 * g + 2 * j])), at(at_z(OFF[4 * g + 2 * j + 1])))
                                 for j in range(2)], axis=1) for g in range(2)]

    lse = in_order(lambda i: lsum[pl.ds(i, 1), :])
    pairs = [p - z * 2048 for p in in_order(lambda i: pbuf[i])]

    FAC = SCALE / BATCH
    zq = zqa[...].reshape(NZ * OWN, EMB)
    row = lax.broadcasted_iota(jnp.int32, (256, 256), 0)
    core_row = (row // 128) * 64 + row % 32
    peer_row = (row // 32) % 4
    pos = []

    def weights_of(g):
        total = jnp.zeros((1, 256), F32)
        for h in range(2):
            ids = core_row + peer_row * (128, 512)[h] + 32 * h

            def weight_step(a, total, h=h, ids=ids):
                v = st[g, h * 4 + a]
                hit = ids == pairs[g] - a * (512, 128)[h]
                e = jnp.exp(v - lse[g])
                wt[h * 4 + a, :, 256 * g:256 * g + 256] = jnp.where(hit, e - 1.0, e).astype(BF16)
                return total + jnp.sum(jnp.where(hit, v, 0.0), axis=0, keepdims=True)

            total = lax.fori_loop(0, 4, weight_step, total)
        pos.append(total)

    weights_of(1)
    def query_rows(g):
        wg = wt[:, :, 256 * g:256 * g + 256].reshape(2048, 256)
        v = lax.dot_general(wg, zka[...].reshape(2048, EMB), TN, preferred_element_type=F32) * FAC
        dqf[pl.ds(4 * g, 4)] = v.reshape(4, OWN, EMB)

    query_rows(1)
    def ahead(dr, d):
        return d if dr == 0 else NZ - d

    zc = {}
    for dr in range(2):
        zs[dr, 1, H[dr], :] = dqf[SLOT[4], H[dr], :].astype(BF16)
        zc[dr, 1] = send(zs.at[dr, 1, H[dr]], zr.at[dr, 1, H[dr]], z_dev[ahead(dr, 2)])
    for n in range(2):
        for dr in range(2):
            h = H[1 - dr if n == 0 else dr]
            zs[dr, 0, h, :] = dqf[SLOT[ahead(dr, 3)], h, :].astype(BF16)
            zc[dr, 0, n] = send(zs.at[dr, 0, h], zr.at[dr, 0, h], z_dev[ahead(dr, 1)])
    weights_of(0)

    kcs = {}

    def key_rows(d, h):
        a = turn[h](d)
        v = jnp.dot(wt[h * 4 + a], zq, preferred_element_type=F32) * FAC
        dk[h, a] = v.astype(BF16).reshape(2, 4, HALF, EMB)
        kcs[d, h] = send(dk.at[h, a, oc], ck.at[h, a], core_dev)

    k1c = ([], [])

    def core_sum(d, h):
        a = turn[h](d)
        kcs[d, h].wait_recv()
        v = (dk[h, a, c].astype(F32) + ck[h, a].astype(F32)).astype(BF16)
        if d:
            pk[h, a] = v
            k1c[h].append(send(pk.at[h, a], k1.at[h, home[h]], second[h][d]))
        else:
            k1[h, a] = v

    steps = [(d, h) for d in (2, 1, 3, 0) for h in range(2)]
    for n, (d, h) in enumerate(steps):
        key_rows(d, h)
        if n >= 3:
            core_sum(*steps[n - 3])
    for n in (5, 6, 7):
        core_sum(*steps[n])
    query_rows(0)
    for dr in range(2):
        zs[dr, 2] = dqf[SLOT[ahead(dr, 1)]].astype(BF16)
        zc[dr, 2] = send(zs.at[dr, 2], zr.at[dr, 2], z_dev[ahead(dr, 1)])
    lanes0 = jnp.where(low, lse[0][:, :128], 0.0)
    l1[t] = lanes0 - add_all([p[:, 128 * j:128 * j + 128] for p in pos for j in range(2)])
    lo1 = [send(l1.at[t], l1.at[t], p) for p in (core_dev, partner, cross)]
    for n in range(2):
        for dr in range(2):
            h = H[1 - dr if n == 0 else dr]
            zc[dr, 0, n].wait_recv()
            v = dqf[SLOT[ahead(dr, 2)], h, :] + zr[dr, 0, h, :].astype(F32)
            if n == 1:
                zc[dr, 1].wait_recv()
                v += zr[dr, 1, h, :].astype(F32)
            zs[dr, 3, h, :] = v.astype(BF16)
            zc[dr, 3, n] = send(zs.at[dr, 3, h], zr.at[dr, 3, h], z_dev[ahead(dr, 2)])
    k2c = []
    for h in range(2):
        for cp in k1c[h]:
            cp.wait_recv()
        k2s[h] = add_all([k1[h, i].astype(F32) for i in range(4)]).astype(BF16)
        me = home[1 - h]
        k2c += [send(k2s.at[h, turn[1 - h](d)], k2.at[h, me], first[h][d]) for d in NEAR]
        k2[h, me] = k2s[h, me]
    for dr in range(2):
        zc[dr, 2].wait_recv()
    for n in range(2):
        for dr in range(2):
            zc[dr, 3, n].wait_recv()
    q1, q2, q3 = [], [], []
    for h in range(2):
        dq4[t, H[h], :] = (dqf[0, H[h], :] + add_all(
            [zr[dr, i, H[h], :].astype(F32) for dr in range(2) for i in (2, 3)])).astype(BF16)
        r = dq4.at[t, H[h]]
        q1.append(send(r, r, partner))
        q2.append(send(r, r, core_dev))
        q3.append(send(r, r, cross))
    d1, d2, d3 = [], [], []
    for h in range(2):
        for cp in k2c[3 * h:3 * h + 3]:
            cp.wait_recv()
        dk4[t, H[h], :] = add_all([k2[h, i].astype(F32) for i in range(4)]).astype(BF16)
        r = dk4.at[t, H[h]]
        d1.append(send(r, r, partner))
        d2.append(send(r, r, core_dev))
        d3.append(send(r, r, cross))
    for cp in q1 + q2 + q3:
        cp.wait_recv()
    dq = dq4[...].reshape(ROWS, EMB)
    head = jnp.dot(xqt[...], dq, preferred_element_type=F32)
    for cp in d1 + d2 + d3:
        cp.wait_recv()
    dkv = dk4[...].reshape(ROWS, EMB)
    head += jnp.dot(xkt[...], dkv, preferred_element_type=F32)

    for i in range(4):
        for j in range(2):
            gs[i, j] = head[i * 48:(i + 1) * 48, j * 256:(j + 1) * 256].astype(BF16)
    plane = [(diag[2], at_y(2), oxh), (diag[1], at_y(1), oxh), (diag[3], at_y(3), oxh), (y_dev[2], at_y(2), xh),
             ({"xh": oxh}, y, oxh), (y_dev[1], at_y(1), xh), (y_dev[3], at_y(3), xh)]
    sent = len(copies)
    h1 = [send(gs.at[py, px], g1r.at[y, xh], p) for p, py, px in plane]
    for cp in lo1:
        cp.wait_recv()
    l2[y, xh] = l1[0] + l1[1] + l1[2] + l1[3]
    lo2 = [send(l2.at[y, xh], l2.at[y, xh], p) for p, py, px in plane]
    gq_h[...] = lax.dot_general(w[...], dq, NT, preferred_element_type=F32).astype(BF16)
    gk_h[...] = lax.dot_general(w[...], dkv, NT, preferred_element_type=F32).astype(BF16)
    g1r[y, xh] = gs[y, xh]
    settle(sent)
    for cp in h1:
        cp.wait_recv()
    order = [(i, j) for i in range(4) for j in range(2)]
    g2r[z] = add_all([g1r[i, j].astype(F32) for i, j in order]).astype(BF16)
    sent = len(copies)
    h2 = [send(g2r.at[z], g2r.at[z], z_dev[d]) for d in FAR]
    for cp in lo2:
        cp.wait_recv()
    l3[z] = add_all([l2[i, j] for i, j in order])
    lo3 = [send(l3.at[z], l3.at[z], z_dev[d]) for d in FAR]
    settle(sent)
    for cp in h2:
        cp.wait_recv()
    g3s[...] = add_all([g2r[i].astype(F32) for i in range(NZ)]).astype(BF16)
    g3r[y, xh] = g3s[...]
    sent = len(copies)
    h3 = [send(g3s, g3r.at[y, xh], p) for p, py, px in plane]
    for cp in lo3:
        cp.wait_recv()
    row = add_all([l3[i] for i in range(NZ)])
    loss_o[...] = jnp.broadcast_to(jnp.sum(row, axis=1, keepdims=True) / BATCH, (1, 128))
    settle(sent)
    for cp in h3:
        cp.wait_recv()
    for i, j in order:
        gh_o[i * 48:(i + 1) * 48, j * 256:(j + 1) * 256] = g3r[i, j].astype(F32)
    settle(len(copies))


def body(query_feat, key_feat, head_weight, pair):
    vmem = pl.BlockSpec(memory_space=pltpu.VMEM)
    hbm = pl.BlockSpec(memory_space=pl.ANY)
    V = pltpu.VMEM
    loss, gq, gk, gh = pl.pallas_call(
        kernel,
        out_shape=(
            jax.ShapeDtypeStruct((1, 128), F32),
            V((FEAT, ROWS), BF16),
            V((FEAT, ROWS), BF16),
            V((FEAT, EMB), F32),
        ),
        in_specs=[hbm] * 4,
        out_specs=(vmem, vmem, vmem, vmem),
        scratch_shapes=[
            V((FEAT, ROWS), BF16), V((FEAT, ROWS), BF16),
            V((ROWS, FEAT), BF16), V((ROWS, FEAT), BF16), V((FEAT, EMB), BF16), V((2, 128), jnp.int32),
            V((4, 2, OWN, FEAT), BF16), V((4, FEAT, EMB), BF16),
            V((NZ, 1, 128), jnp.int32),
            V((NZ, OWN, EMB), BF16), V((2, 4, 2, 4, HALF, EMB), BF16),
            V((2, 8, 256, 256), F32), V((8, 256, 512), BF16),
            V((NZ, NZ, 128), F32), V((NZ, 128), F32),
            V((NZ, OWN, EMB), F32), V((2, 4, OWN, EMB), BF16), V((2, 4, OWN, EMB), BF16),
            V((2, 4, 2, 4, HALF, EMB), BF16), V((2, 4, 4, HALF, EMB), BF16), V((2, 4, 4, HALF, EMB), BF16),
            V((2, 4, 4, HALF, EMB), BF16), V((2, 4, HALF, EMB), BF16), V((2, 4, HALF, EMB), BF16),
            V((4, OWN, EMB), BF16), V((4, OWN, EMB), BF16),
            V((4, 2, 48, 256), BF16), V((4, 2, 48, 256), BF16),
            V((NZ, 48, 256), BF16), V((48, 256), BF16), V((4, 2, 48, 256), BF16),
            V((4, 1, 128), F32), V((4, 2, 1, 128), F32), V((NZ, 1, 128), F32),
            pltpu.SemaphoreType.DMA((N_SEMS,)), pltpu.SemaphoreType.DMA((N_SEMS,)), pltpu.SemaphoreType.DMA((4,)),
        ],
        compiler_params=pltpu.CompilerParams(collective_id=0, has_side_effects=True, vmem_limit_bytes=44 << 20),
    )(*[pltpu.with_memory_space_constraint(v, pltpu.HBM) for v in (
        query_feat.T, key_feat.T, head_weight, pair.reshape(2, 128))])
    return loss[0, 0], gq.T, gk.T, gh


def solution(mesh):
    shape = {"tp": (2, 2), "blk": (8, 4, 2)}
    names = {"tp": TP, "blk": BLK}
    a, b = mesh.axis_names
    fine = Mesh(mesh.devices.reshape(shape[a] + shape[b]), names[a] + names[b])
    in_specs = (P(BLK, TP), P(BLK, TP), P(TP, None), P(BLK))
    out_specs = (P(), P(BLK, TP), P(BLK, TP), P(TP, None))
    return jax.shard_map(body, mesh=fine, in_specs=in_specs, out_specs=out_specs, check_vma=False)
```
